256 devices in a mesh: ctx: 8 (over x_hi, y), fsdp: 32 (over x_lo, z, core).
Axes of the slice: x: 4 (x_hi: 2, x_lo: 2; x = x_hi * 2 + x_lo), y: 4, z: 8, core: 2. Of those that a mesh axis runs over, the one named last changes fastest.
Arguments:
- base_ids: int32 [3072], P('ctx'), may hold values from 0 to 511
- embedding: bfloat16 [512, 8192], P(None, 'fsdp'), may hold values from -3 to 3
- first_gain: float32 [8192], replicated, may hold values from 0.1 to 1.9
- hyena_weight: bfloat16 [8192, 3, 8192], P('ctx', None, 'fsdp'), may hold values from -0.0625 to 0.0625
- short_filter: float32 [3, 3, 8192], P(None, None, 'fsdp'), may hold values from -3 to 3
- long_filter: float32 [128, 8192], P(None, 'fsdp'), may hold values from -0.5 to 0.5
- second_gain: float32 [8192], replicated, may hold values from 0.1 to 1.9
- attn_weight: bfloat16 [8192, 3, 8192], P('ctx', None, 'fsdp'), may hold values from -0.0625 to 0.0625
Outputs:
- mixed: bfloat16 [3072, 8192], P('ctx', 'fsdp')
- attended: bfloat16 [3072, 8192], P('ctx', 'fsdp')
The draws below stay inside these ranges and needn't reach their ends.
All inputs are finite; a program needn't handle non-finite values.
Results may differ from the reference program's by a relative error of at most 0.02.
Values may be sent and summed in bfloat16 or wider, within the bound.
A program may use at most 64 MiB of HBM per device.

```python
import math
import jax
import jax.numpy as jnp
import numpy as np
from jax import lax

D = 8192
VOCAB = 512
HEAD = 128
SHORT = 3
LONG = 128
TOKENS = 3072


def touch_ends(drawn, rng, low, top_value):
    index_at = [jax.random.randint(jax.random.fold_in(rng, axis), (), 0, length) for axis, length in enumerate(drawn.shape)]
    main_axis = drawn.shape.index(max(drawn.shape))
    beside = index_at[:main_axis] + [(index_at[main_axis] + 1) % drawn.shape[main_axis]] + index_at[main_axis + 1:]
    return drawn.at[tuple(index_at)].set(low).at[tuple(beside)].set(top_value)


def block_scale(key, shape, pieces, smallest, largest):
    gain, own = 1.0, jax.random.fold_in(key, 6)
    for dim, parts in pieces:
        draws = jnp.exp(jax.random.uniform(jax.random.fold_in(own, dim), (parts,), jnp.float32, smallest / len(pieces), largest / len(pieces)))
        gain = gain * jnp.repeat(draws, shape[dim] // parts).reshape([-1 if axis == dim else 1 for axis in range(len(shape))])
    return gain


def rank_bounds(count, skew):
    portions = [(1 << 20) // math.isqrt(standing ** skew) + 1 for standing in range(1, count + 1)]
    width = 1 + sum(portions) // (1 << 30)
    return np.cumsum(np.array([max(1, weight // width) for weight in portions]))


def ranked_ids(own_key, dims, number_of, skew):
    table = rank_bounds(number_of, skew)
    pick = jax.random.randint(jax.random.fold_in(own_key, 1), dims, 0, int(table[number_of - 1]))
    rank = jnp.searchsorted(jnp.asarray(table, jnp.int32), pick, side="right")
    return jax.random.permutation(jax.random.fold_in(own_key, 2), number_of)[rank].astype(jnp.int32)


def scatter_about(own_key, extent, spread, limit, pieces=(), kind=jnp.bfloat16):
    values = jax.random.normal(own_key, extent, jnp.float32) * spread
    if len(pieces) > 0:
        values = block_scale(own_key, extent, pieces, -0.22, 0.18) * values
    return jnp.clip(values, min=-limit, max=limit).astype(kind)


def setup_inputs(seed: int = 0) -> dict:
    arg_keys = jax.random.split(jax.random.key(seed), 9)
    base_ids = touch_ends(ranked_ids(arg_keys[0], (TOKENS,), VOCAB, 2), jax.random.fold_in(arg_keys[0], 3), 0, VOCAB - 1).astype(jnp.int32)
    embedding = scatter_about(arg_keys[1], (VOCAB, D), 0.5, 3.0, ((1, 32),))
    first_gain = jnp.clip(1.0 + 0.18 * jax.random.normal(arg_keys[2], (D,), jnp.float32), 0.1, 1.9)
    hyena_weight = scatter_about(arg_keys[3], (D, 3, D), D ** -0.5, 0.0625, ((0, 8), (2, 32)))
    short_filter = scatter_about(arg_keys[4], (SHORT, 3, D), 0.5, 3.0, ((2, 32),), jnp.float32)
    long_filter = scatter_about(arg_keys[5], (LONG, D), LONG ** -0.5, 0.5, ((1, 32),), jnp.float32)
    second_gain = jnp.clip(1.0 + 0.18 * jax.random.normal(arg_keys[6], (D,), jnp.float32), 0.1, 1.9)
    attn_weight = scatter_about(arg_keys[7], (D, 3, D), D ** -0.5, 0.0625, ((0, 8), (2, 32)))
    return {"base_ids": base_ids, "embedding": embedding, "first_gain": first_gain, "hyena_weight": hyena_weight, "short_filter": short_filter, "long_filter": long_filter, "second_gain": second_gain, "attn_weight": attn_weight}


def norm_rows(values, gain_vector):
    values = values.astype(jnp.float32)
    factor = lax.rsqrt(lax.optimization_barrier(jnp.mean(values * values, axis=-1, keepdims=True)) + 1e-06)
    return values * factor * gain_vector.astype(jnp.float32)

def head_norm(values):
    values = values.astype(jnp.float32)
    return values * lax.rsqrt(lax.optimization_barrier(jnp.mean(values * values, axis=-1, keepdims=True)) + 1e-06)

def causal_filter(values, kernel):
    lag_count = kernel.shape[0]
    length = values.shape[0]
    padded = jnp.concatenate([jnp.zeros((lag_count - 1,) + values.shape[1:], jnp.float32), values], axis=0)

    def step(running, lag_index):
        window = lax.dynamic_slice_in_dim(padded, (lag_count - 1 - lag_index).astype(jnp.int32), length, 0)
        coefficient = lax.dynamic_index_in_dim(kernel, lag_index, 0, keepdims=False)
        return (running + coefficient * window, None)
    running, _ = lax.scan(step, jnp.zeros_like(values), jnp.arange(lag_count, dtype=jnp.int32))
    return running

def reference(base_ids, embedding, first_gain, hyena_weight, short_filter, long_filter, second_gain, attn_weight):
    length = base_ids.shape[0]
    features = embedding[base_ids]
    normed = norm_rows(features, first_gain).astype(jnp.bfloat16)
    streams = jnp.dot(normed, hyena_weight.reshape(D, 3 * D), preferred_element_type=jnp.float32)
    streams = streams.reshape(length, 3, D).astype(jnp.bfloat16)
    filtered = causal_filter(streams.astype(jnp.float32), short_filter.astype(jnp.float32))
    product = (filtered[:, 1, :] * filtered[:, 2, :]).astype(jnp.bfloat16)
    longconv = causal_filter(product.astype(jnp.float32), long_filter.astype(jnp.float32))
    mixed = (features.astype(jnp.float32) + filtered[:, 0, :] * longconv).astype(jnp.bfloat16)
    renormed = norm_rows(mixed, second_gain).astype(jnp.bfloat16)
    triple = jnp.dot(renormed, attn_weight.reshape(D, 3 * D), preferred_element_type=jnp.float32)
    triple = triple.reshape(length, 3, D).astype(jnp.bfloat16)
    head_count = D // HEAD
    unit_q = head_norm(triple[:, 0, :].reshape(length, head_count, HEAD)).astype(jnp.bfloat16)
    unit_k = head_norm(triple[:, 1, :].reshape(length, head_count, HEAD)).astype(jnp.bfloat16)
    values_in = triple[:, 2, :].reshape(length, head_count, HEAD)
    positions = jnp.arange(length, dtype=jnp.int32)
    allowed = positions[None, :] <= positions[:, None]
    score_factor = 2.0 * HEAD ** (-0.5)

    def one_head(item):
        query_block, key_block, value_block = item
        score = jnp.dot(query_block, key_block.T, preferred_element_type=jnp.float32) * score_factor
        weight = jnp.where(allowed, jnp.exp(score), 0.0)
        total = lax.optimization_barrier(jnp.sum(weight, axis=1))
        numerator = jnp.dot(weight.astype(jnp.bfloat16), value_block, preferred_element_type=jnp.float32)
        return (numerator / total[:, None]).astype(jnp.bfloat16)
    outputs = lax.map(one_head, (jnp.transpose(unit_q, (1, 0, 2)), jnp.transpose(unit_k, (1, 0, 2)), jnp.transpose(values_in, (1, 0, 2))))
    attended = jnp.transpose(outputs, (1, 0, 2)).reshape(length, D)
    return (mixed, attended)
```

```python
import functools

import jax
import jax.numpy as jnp
from jax import lax
from jax.experimental import pallas as pl
from jax.experimental.pallas import tpu as pltpu
from jax.sharding import PartitionSpec as P

MESH = pl.DeviceIdType.MESH
F32, BF16 = jnp.float32, jnp.bfloat16
T = 384
V = 512
C = 256
KD = 1024
D = 8192
HEAD = 128
LONG = 128
EPS = 1e-6
HALF = T // 2


def dot(a, b):
    return jnp.dot(a, b, preferred_element_type=F32)


def split_pair(values):
    high = values.astype(BF16)
    low = (values - high.astype(F32)).astype(BF16)
    lanes = lax.broadcasted_iota(jnp.int32, (values.shape[0], 128), 1)
    wide = jnp.where(lanes < 64, high.astype(F32), low.astype(F32))
    return wide.astype(BF16)


def join_pair(wide):
    wide = wide.astype(F32)
    return wide[:, 0:1] + wide[:, 64:65]


def kernel(
    ids, emb, g1, w1, sf, lf, g2, w2,
    mixed_out, att_out,
    idbuf, ebuf, xbuf, pbuf, rsbuf, tbuf, sbuf, prbuf, ext, lcbuf, mbuf,
    w2all, mall, pp, ssb, gs, gr, qbuf, kvall, oloc, obuf,
    id_s, id_r, sc_s, sc_r, az_s, az_r, ax_s, ax_r, ac_s, ac_r,
    rs_s, rs_r, ag_s, ag_r, w_s, w_r, e1_s, e1_r, zr_s, zr_r, zl_s, zl_r, sib_s, sib_r,
    g_s, g_r, kv_s, kv_r, o_s, o_r,
):
    c = lax.axis_index("ctx")
    f = lax.axis_index("fsdp")
    xh, y = c // 4, c % 4
    xl, z, k = f // 16, (f // 2) % 8, f % 2

    def dev(xh_, y_, xl_, z_, k_):
        return (xh_ * 4 + y_, xl_ * 16 + z_ * 2 + k_)

    def ctx_peer(d):
        return ((c + d) % 8, f)

    def z_peer(d):
        return dev(xh, y, xl, (z + d) % 8, k)

    def y_peer(d):
        return dev(xh, (y + d) % 4, xl, z, k)

    x_sib = dev(xh, y, 1 - xl, z, k)
    core_sib = dev(xh, y, xl, z, 1 - k)
    x_far = dev(1 - xh, y, xl, z, k)

    def remote(src, dst, ss, rs, to):
        return pltpu.make_async_remote_copy(
            src_ref=src, dst_ref=dst, send_sem=ss, recv_sem=rs, device_id=to, device_id_type=MESH
        )

    barrier = pltpu.get_barrier_semaphore()
    count = 0
    peers = [ctx_peer(d) for d in range(1, 8)] + [z_peer(d) for d in range(1, 8)] + [x_sib, core_sib]
    peers += [dev(xl, z // 2, xh, 2 * y + e, k) for e in range(2)]
    peers += [dev(xl, y, a, z, k) for a in range(2)]
    peers += [dev(a, y, xh, z, k) for a in range(2)]
    for p in peers:
        pl.semaphore_signal(barrier, inc=1, device_id=p, device_id_type=MESH)
        count += 1
    pl.semaphore_wait(barrier, count)

    def id_copy():
        return remote(ids, idbuf, id_s, id_r, ctx_peer(1))

    @pl.when(c < 7)
    def _():
        id_copy().start()

    rows_of = lambda xl_, z_: pl.ds(pl.multiple_of(xl_ * 256 + z_ * 32, 32), 32)

    def sc_copy(e):
        rows = rows_of(xh, 2 * y + e)
        cols = pl.ds(pl.multiple_of((z % 2) * C, C), C)
        src, dst = emb.at[rows, :], ebuf.at[k, rows, cols]
        return src, dst, remote(src, dst, sc_s.at[e], sc_r.at[z % 2], dev(xl, z // 2, xh, 2 * y + e, k))

    for e in range(2):
        src, dst, cp = sc_copy(e)
        me = (xl == xh) & (z // 2 == y) & (2 * y + e == z)

        @pl.when(me)
        def _():
            pltpu.make_async_copy(src, dst, sc_r.at[z % 2]).start()

        @pl.when(jnp.logical_not(me))
        def _():
            cp.start()

    def w_copy(d):
        slot = {1: 0, -1: 1}[d]
        return remote(w2, w2all.at[y], w_s.at[slot], w_r.at[slot], y_peer(d))

    def w_forward(d):
        slot = {1: 2, -1: 3}[d]
        half = {1: 0, -1: 1}[d]
        part = w2all.at[(y - d) % 4, :, pl.ds(half * (KD // 2), KD // 2), :]
        return remote(part, part, w_s.at[slot], w_r.at[slot], y_peer(d))

    w_copy(1).start()
    w_copy(-1).start()
    w_local = pltpu.make_async_copy(w2, w2all.at[y], w_s.at[4])
    w_local.start()

    for zb in range(2):
        rows = rows_of(xl, z)
        piece = ebuf.at[k, rows, pl.ds(zb * C, C)]
        remote(piece, piece, sc_s.at[zb], sc_r.at[zb], core_sib).wait_recv()

    def az_copy(d):
        piece = ebuf.at[k, rows_of(xl, z), :]
        return remote(piece, piece, az_s.at[d], az_r.at[d], z_peer(d))

    def ax_copy(d):
        piece = ebuf.at[k, rows_of(xl, (z - d) % 8), :]
        return remote(piece, piece, ax_s.at[d], ax_r.at[d], x_sib)

    def ac_copy(d, s):
        xl_ = (xl + s) % 2
        piece = ebuf.at[k, rows_of(xl_, (z - d) % 8), :]
        return remote(piece, piece, ac_s.at[s, d], ac_r.at[s, d], core_sib)

    order = (1, 7, 2, 6, 3, 5, 4)
    for d in order:
        az_copy(d).start()
    ax_copy(0).start()
    ac_copy(0, 0).start()
    for d in order:
        az_copy(d).wait_recv()
        ax_copy(d).start()
        ac_copy(d, 0).start()
    for d in (0,) + order:
        ax_copy(d).wait_recv()
        ac_copy(d, 1).start()
    for d in (0,) + order:
        ac_copy(d, 0).wait_recv()
        ac_copy(d, 1).wait_recv()

    gain = g1[pl.ds(c, 1), :]
    squares = jnp.zeros((V, 1), F32)
    for q in range(4):
        e = ebuf[q % 2, :, (q // 2) * C : (q // 2 + 1) * C].astype(F32)
        squares = squares + jnp.sum(e * e, axis=1, keepdims=True)
        xbuf[:, q * C : (q + 1) * C] = (e * gain[:, q * C : (q + 1) * C]).astype(BF16)
    pbuf[:, 3 * C : 3 * C + 128] = split_pair(squares)
    for m in range(3):
        pbuf[:, m * C : (m + 1) * C] = dot(xbuf[...], w1[m]).astype(BF16)

    def rs_copy(d):
        rows = pl.ds(pl.multiple_of(((c + d) % 8) * 64, 64), 64)
        return remote(pbuf.at[rows, :], rsbuf.at[d - 1], rs_s.at[d - 1], rs_r.at[d - 1], ctx_peer(d))

    def ag_copy(d):
        rows = pl.ds(pl.multiple_of(c * 64, 64), 64)
        return remote(tbuf.at[rows, :], tbuf.at[rows, :], ag_s.at[d - 1], ag_r.at[d - 1], ctx_peer(d))

    for d in range(1, 8):
        rs_copy(d).start()
    mine = pl.ds(pl.multiple_of(c * 64, 64), 64)
    total = pbuf[mine, : 3 * C].astype(F32)
    sq = join_pair(pbuf[mine, 3 * C :])
    for d in range(1, 8):
        rs_copy(d).wait_recv()
        total = total + rsbuf[d - 1, :, : 3 * C].astype(F32)
        sq = sq + join_pair(rsbuf[d - 1, :, 3 * C :])
    tbuf[mine, :] = (total * lax.rsqrt(sq / D + EPS)).astype(BF16)
    for d in range(1, 8):
        ag_copy(d).start()

    @pl.when(c > 0)
    def _():
        id_copy().wait_recv()

    @pl.when(c == 0)
    def _():
        idbuf[...] = jnp.full(idbuf.shape, -1, jnp.int32)

    for d in range(1, 8):
        ag_copy(d).wait_recv()

    w_copy(1).wait_recv()
    w_forward(1).start()
    w_copy(-1).wait_recv()
    w_forward(-1).start()

    def one_hot(chunk):
        row = idbuf[:, 128 + chunk * 128 : 256 + chunk * 128] if chunk < 2 else ids[:, (chunk - 2) * 128 : (chunk - 1) * 128]
        words = lax.broadcasted_iota(jnp.int32, (V, 128), 0)
        return jnp.where(words == row, 1.0, 0.0).astype(BF16)

    def pick(hot, values):
        return lax.dot_general(hot, values, (((0,), (0,)), ((), ())), preferred_element_type=F32)

    for chunk in range(5):
        sbuf[chunk * 128 : (chunk + 1) * 128, :] = pick(one_hot(chunk), tbuf[...])

    def short(m, start, size):
        cols = slice(m * C, (m + 1) * C)
        out = sf[m : m + 1, :] * sbuf[start : start + size, cols]
        for j in range(1, 3):
            out = out + sf[3 * j + m : 3 * j + m + 1, :] * sbuf[start - j : start - j + size, cols]
        return out

    for chunk in range(4):
        prod = (short(1, 128 + chunk * 128, 128) * short(2, 128 + chunk * 128, 128)).astype(BF16).astype(F32)
        for lt in range(2):
            prbuf[lt, chunk * 128 : (chunk + 1) * 128, :] = prod[:, lt * 128 : (lt + 1) * 128]

    LANE_T = T // 8
    for lt in range(2):

        @pl.loop(0, LANE_T + LONG - 1)
        def _(i):
            ext[lt, i] = prbuf[lt, pl.ds(i + 1, 8, stride=LANE_T), :]

    for lt in range(2):
        for ig in range(3):

            def taps(j8, acc):
                window = ext[lt, pl.ds(ig * 16 + 120 - 8 * j8, 23)]
                coef = lf[pl.ds(pl.multiple_of(8 * j8, 8), 8), lt * 128 : (lt + 1) * 128]
                for jj in range(8):
                    acc = acc + coef[jj : jj + 1, :][None] * window[7 - jj : 23 - jj]
                return acc

            acc = lax.fori_loop(0, LONG // 8, taps, jnp.zeros((16, 8, 128), F32))
            for ii in range(16):
                lcbuf[lt, pl.ds(ig * 16 + ii, 8, stride=LANE_T), :] = acc[ii]

    for chunk in range(3):
        rows = slice(chunk * 128, (chunk + 1) * 128)
        features = pick(one_hot(chunk + 2), emb[...])
        gate = short(0, 256 + chunk * 128, 128)
        for lt in range(2):
            cols = slice(lt * 128, (lt + 1) * 128)
            mixed = (features[:, cols] + gate[:, cols] * lcbuf[lt, rows, :]).astype(BF16)
            mbuf[rows, cols] = mixed
            mixed_out[rows, cols] = mixed

    def cols_of(z_, k_):
        return pl.ds(pl.multiple_of((z_ * 2 + k_) * C, C), C)

    def e1_copy(a):
        dst = mall.at[xh, :, cols_of(z, k)]
        return dst, remote(mbuf, dst, e1_s.at[a], e1_r.at[xh], dev(xl, y, a, z, k))

    for a in range(2):
        dst, cp = e1_copy(a)
        me = (xl == xh) & (xl == a)

        @pl.when(me)
        def _():
            pltpu.make_async_copy(mbuf, dst, e1_r.at[xh]).start()

        @pl.when(jnp.logical_not(me))
        def _():
            cp.start()

    def chunk_of(b, z_, k_, h):
        return mall.at[b, h * HALF : (h + 1) * HALF, cols_of(z_, k_)]

    def zr_copy(b, s, h):
        piece = chunk_of(b, (z - s) % 8, k, h)
        return remote(piece, piece, zr_s.at[b, s, h], zr_r.at[b, s, h], z_peer(1))

    def zl_copy(b, s, h):
        piece = chunk_of(b, (z + s) % 8, k, h)
        return remote(piece, piece, zl_s.at[b, s, h], zl_r.at[b, s, h], z_peer(-1))

    def sib_copy(b, s, h):
        piece = chunk_of(b, (z + s) % 8, k, h)
        return remote(piece, piece, sib_s.at[b, s, h], sib_r.at[b, s, h], core_sib)

    def ring(b):
        piece = mall.at[b, :, cols_of(z, k)]
        remote(piece, piece, e1_s.at[0], e1_r.at[b], core_sib).wait_recv()
        for h in range(2):
            zr_copy(b, 0, h).start()
            zl_copy(b, 0, h).start()
        for h in range(2):
            sib_copy(b, 0, h).start()
        for s in range(1, 5):
            for h in range(2):
                if s < 4 or h == 0:
                    zr_copy(b, s - 1, h).wait_recv()
                    if s < 3 or (s == 3 and h == 0):
                        zr_copy(b, s, h).start()
                    sib_copy(b, 8 - s, h).start()
                if s < 4 or h == 1:
                    zl_copy(b, s - 1, h).wait_recv()
                    if s < 3 or (s == 3 and h == 1):
                        zl_copy(b, s, h).start()
                    sib_copy(b, s, h).start()

    def ring_end(b):
        for s in range(8):
            for h in range(2):
                sib_copy(b, s, h).wait_recv()

    ring(0)
    ring(1)
    ring_end(0)
    ring_end(1)
    w_local.wait()
    w_forward(1).wait_recv()
    w_forward(-1).wait_recv()

    def project(b):
        pp[b] = jnp.zeros(pp.shape[1:], F32)
        ssb[b] = jnp.zeros(ssb.shape[1:], F32)

        @pl.loop(0, 4)
        def _(ys):
            scale = g2[pl.ds(4 * xh + ys, 1), :]
            cols = pl.ds(pl.multiple_of(ys * KD, KD), KD)
            for r in range(3):
                rows = slice(r * 128, (r + 1) * 128)
                part = mall[b, rows, cols].astype(F32)
                ssb[b, rows, :] += jnp.sum(part * part, axis=1, keepdims=True)
                xbuf[rows, :] = (part * scale).astype(BF16)
            for m in range(3):
                pp[b, :, m * C : (m + 1) * C] += dot(xbuf[:T, :], w2all[ys, m])

    def g_copy(b):
        return remote(gs.at[b], gr.at[b], g_s.at[b], g_r.at[b], x_far)

    def head_cols(m, h):
        return pl.ds(pl.multiple_of(m * C + h * HEAD, HEAD), HEAD)

    def send_half(b):
        for m in range(3):
            gs[b, m] = pp[b, :, head_cols(m, 1 - xh)].astype(BF16)
        gs[b, 3] = split_pair(ssb[b, :, 0:1])
        g_copy(b).start()

    def head_norm(values):
        values = values.astype(F32)
        return (values * lax.rsqrt(jnp.mean(values * values, axis=1, keepdims=True) + EPS)).astype(BF16)

    def kv_copy(b, d):
        block = kvall.at[y, b]
        return remote(block, block, kv_s.at[b, d - 1], kv_r.at[b, d - 1], y_peer(d))

    def finish(b):
        g_copy(b).wait_recv()
        row = lax.rsqrt((ssb[b, :, 0:1] + join_pair(gr[b, 3])) / D + EPS)
        triple = [((pp[b, :, head_cols(m, xh)] + gr[b, m].astype(F32)) * row).astype(BF16) for m in range(3)]
        kvall[y, b, 0] = head_norm(triple[1])
        kvall[y, b, 1] = triple[2]
        for d in range(1, 4):
            kv_copy(b, d).start()
        qbuf[b] = head_norm(triple[0])

    project(0)
    send_half(0)
    project(1)
    send_half(1)
    finish(0)
    finish(1)
    for b in range(2):
        for d in range(1, 4):
            kv_copy(b, d).wait_recv()

    factor = 2.0 * HEAD ** -0.5

    def attend(b):
        @pl.loop(0, 3)
        def _(qc):
            rows = pl.ds(pl.multiple_of(qc * 128, 128), 128)
            query = qbuf[b, rows, :]

            def weights(ys, kb):
                score = lax.dot_general(
                    query, kvall[ys, kb, 0], (((1,), (1,)), ((), ())), preferred_element_type=F32
                )
                return jnp.exp(score * factor)

            def add(carry, weight, ys, kb):
                num, den = carry
                den = den + jnp.sum(weight, axis=1, keepdims=True)
                return num + dot(weight.astype(BF16), kvall[ys, kb, 1]), den

            def full(kb):
                return lambda ys, carry: add(carry, weights(ys, kb), ys, kb)

            carry = (jnp.zeros((128, HEAD), F32), jnp.zeros((128, 1), F32))
            if b == 1:
                carry = lax.fori_loop(0, 4, full(0), carry)
            carry = lax.fori_loop(0, y, full(b), carry)
            weight = weights(y, b)
            at = qc * 128 + lax.broadcasted_iota(jnp.int32, (128, T), 0)
            key = lax.broadcasted_iota(jnp.int32, (128, T), 1)
            weight = jnp.where(key <= at, weight, 0.0)
            num, den = add(carry, weight, y, b)
            oloc[b, rows, :] = (num / den).astype(BF16)

    attend(0)
    attend(1)

    here = pl.ds(pl.multiple_of(xh * HEAD, HEAD), HEAD)
    there = pl.ds(pl.multiple_of((1 - xh) * HEAD, HEAD), HEAD)
    o_copy = remote(oloc.at[1 - xh], obuf, o_s, o_r, x_far)
    o_copy.start()
    att_out[:, here] = oloc[xh]
    o_copy.wait_recv()
    att_out[:, there] = obuf[...]

    @pl.when(c < 7)
    def _():
        id_copy().wait_send()

    for e in range(2):
        me = (xl == xh) & (z // 2 == y) & (2 * y + e == z)

        @pl.when(jnp.logical_not(me))
        def _():
            sc_copy(e)[2].wait_send()

    for a in range(2):
        me = (xl == xh) & (xl == a)

        @pl.when(jnp.logical_not(me))
        def _():
            e1_copy(a)[1].wait_send()

    for d in (1, -1):
        w_copy(d).wait_send()
        w_forward(d).wait_send()
    for d in order:
        az_copy(d).wait_send()
    for d in range(8):
        ax_copy(d).wait_send()
        ac_copy(d, 0).wait_send()
        ac_copy(d, 1).wait_send()
    for d in range(1, 8):
        rs_copy(d).wait_send()
        ag_copy(d).wait_send()
    for b in range(2):
        for s in range(4):
            for h in range(2):
                if s < 3 or h == 0:
                    zr_copy(b, s, h).wait_send()
                if s < 3 or h == 1:
                    zl_copy(b, s, h).wait_send()
        for s in range(8):
            for h in range(2):
                sib_copy(b, s, h).wait_send()
        g_copy(b).wait_send()
        for d in range(1, 4):
            kv_copy(b, d).wait_send()
    o_copy.wait_send()


def local(base_ids, embedding, first_gain, hyena_weight, short_filter, long_filter, second_gain, attn_weight):
    dma = pltpu.SemaphoreType.DMA
    vmem = pltpu.VMEM
    scratch = [
        vmem((1, T), jnp.int32),
        vmem((2, V, 2 * C), BF16),
        vmem((V, KD), BF16),
        vmem((V, 3 * C + 128), BF16),
        vmem((7, 64, 3 * C + 128), BF16),
        vmem((V, 3 * C), BF16),
        vmem((640, 3 * C), F32),
        vmem((2, 512, 128), F32),
        vmem((2, T // 8 + LONG, 8, 128), F32),
        vmem((2, T, 128), F32),
        vmem((T, C), BF16),
        vmem((4, 3, KD, C), BF16),
        vmem((2, T, 16 * C), BF16),
        vmem((2, T, 3 * C), F32),
        vmem((2, T, 128), F32),
        vmem((2, 4, T, HEAD), BF16),
        vmem((2, 4, T, HEAD), BF16),
        vmem((2, T, HEAD), BF16),
        vmem((4, 2, 2, T, HEAD), BF16),
        vmem((2, T, HEAD), BF16),
        vmem((T, HEAD), BF16),
        dma, dma,
        dma((2,)), dma((2,)),
        dma((8,)), dma((8,)),
        dma((8,)), dma((8,)),
        dma((2, 8)), dma((2, 8)),
        dma((7,)), dma((7,)),
        dma((7,)), dma((7,)),
        dma((5,)), dma((4,)),
        dma((2,)), dma((2,)),
        dma((2, 4, 2)), dma((2, 4, 2)),
        dma((2, 4, 2)), dma((2, 4, 2)),
        dma((2, 8, 2)), dma((2, 8, 2)),
        dma((2,)), dma((2,)),
        dma((2, 3)), dma((2, 3)),
        dma, dma,
    ]
    return pl.pallas_call(
        kernel,
        out_shape=(jax.ShapeDtypeStruct((T, C), BF16), jax.ShapeDtypeStruct((T, C), BF16)),
        in_specs=[pl.BlockSpec(memory_space=pltpu.VMEM)] * 8,
        out_specs=(pl.BlockSpec(memory_space=pltpu.VMEM), pl.BlockSpec(memory_space=pltpu.VMEM)),
        scratch_shapes=scratch,
        compiler_params=pltpu.CompilerParams(
            collective_id=0, has_side_effects=True, vmem_limit_bytes=56 << 20
        ),
    )(
        base_ids.reshape(1, T),
        embedding,
        first_gain.reshape(8, KD),
        jnp.transpose(hyena_weight, (1, 0, 2)),
        short_filter.reshape(9, C),
        long_filter,
        second_gain.reshape(8, KD),
        jnp.transpose(attn_weight, (1, 0, 2)),
    )


def solution(mesh):
    return jax.shard_map(
        local,
        mesh=mesh,
        in_specs=(
            P("ctx"),
            P(None, "fsdp"),
            P(),
            P("ctx", None, "fsdp"),
            P(None, None, "fsdp"),
            P(None, "fsdp"),
            P(),
            P("ctx", None, "fsdp"),
        ),
        out_specs=(P("ctx", "fsdp"), P("ctx", "fsdp")),
        check_vma=False,
    )
```

```python
import functools

import jax
import jax.numpy as jnp
from jax import lax
from jax.experimental import pallas as pl
from jax.experimental.pallas import tpu as pltpu
from jax.sharding import PartitionSpec as P

MESH = pl.DeviceIdType.MESH
F32, BF16 = jnp.float32, jnp.bfloat16
T = 384
V = 512
C = 256
KD = 1024
D = 8192
HEAD = 128
LONG = 128
EPS = 1e-6


def dot(a, b):
    return jnp.dot(a, b, preferred_element_type=F32)


def kernel(
    ids, emb, g1, w1, sf, lf, g2, w2,
    mixed_out, att_out,
    idbuf, ebuf, xbuf, pkv, pq, psq, rskv, rsq, rssq, tkv, tq, sbuf, prbuf, ext, lcbuf, mbuf,
    w2all, mall, xs, pp, ssb, gs, gr, sqs, sqr, qbuf, kvall, oloc, obuf,
    id_s, id_r, sc_s, sc_r, az_s, az_r, ax_s, ax_r, ac_s, ac_r,
    rs_s, rs_r, ag_s, ag_r, w_s, w_r, wl_s, e1_s, e1_r, zr_s, zr_r, zl_s, zl_r, sib_s, sib_r,
    g_s, g_r, kv_s, kv_r, o_s, o_r,
):
    c = lax.axis_index("ctx")
    f = lax.axis_index("fsdp")
    xh, y = c // 4, c % 4
    xl, z, k = f // 16, (f // 2) % 8, f % 2

    def dev(xh_, y_, xl_, z_, k_):
        return (xh_ * 4 + y_, xl_ * 16 + z_ * 2 + k_)

    def ctx_peer(d):
        return ((c + d) % 8, f)

    def z_peer(d):
        return dev(xh, y, xl, (z + d) % 8, k)

    def y_peer(d):
        return dev(xh, (y + d) % 4, xl, z, k)

    x_sib = dev(xh, y, 1 - xl, z, k)
    core_sib = dev(xh, y, xl, z, 1 - k)
    x_far = dev(1 - xh, y, xl, z, k)

    def remote(src, dst, ss, rs, to):
        return pltpu.make_async_remote_copy(
            src_ref=src, dst_ref=dst, send_sem=ss, recv_sem=rs, device_id=to, device_id_type=MESH
        )

    barrier = pltpu.get_barrier_semaphore()
    count = 0
    peers = [ctx_peer(d) for d in range(1, 8)] + [z_peer(d) for d in range(1, 8)] + [x_sib, core_sib]
    peers += [dev(xl, z // 2, xh, 2 * y + e, k) for e in range(2)]
    peers += [dev(xl, y, a, z, k) for a in range(2)]
    peers += [dev(a, y, xh, z, k) for a in range(2)]
    for p in peers:
        pl.semaphore_signal(barrier, inc=1, device_id=p, device_id_type=MESH)
        count += 1
    pl.semaphore_wait(barrier, count)

    def id_copy():
        return remote(ids, idbuf, id_s, id_r, ctx_peer(1))

    @pl.when(c < 7)
    def _():
        id_copy().start()

    rows_of = lambda xl_, z_: pl.ds(pl.multiple_of(xl_ * 256 + z_ * 32, 32), 32)

    def sc_copy(e):
        rows = rows_of(xh, 2 * y + e)
        cols = pl.ds(pl.multiple_of((z % 2) * C, C), C)
        src, dst = emb.at[rows, :], ebuf.at[k, rows, cols]
        return src, dst, remote(src, dst, sc_s.at[e], sc_r.at[z % 2], dev(xl, z // 2, xh, 2 * y + e, k))

    for e in range(2):
        src, dst, cp = sc_copy(e)
        me = (xl == xh) & (z // 2 == y) & (2 * y + e == z)

        @pl.when(me)
        def _():
            pltpu.make_async_copy(src, dst, sc_r.at[z % 2]).start()

        @pl.when(jnp.logical_not(me))
        def _():
            cp.start()

    W_PARTS = ((1, 3, 0, KD // 2), (1, 3, KD // 2, KD // 2), (0, 1, 0, KD))

    def w_copy(part, d):
        m0, m1, row, count_ = W_PARTS[part]
        side = {1: 0, -1: 1}[d]
        cut = (slice(m0, m1), slice(row, row + count_), slice(None))
        return remote(
            w2.at[cut], w2all.at[(y,) + cut], w_s.at[part, 0, side], w_r.at[part, 0, side], y_peer(d)
        )

    def w_forward(part, d):
        m0, m1, row, count_ = W_PARTS[part]
        side = {1: 0, -1: 1}[d]
        half = count_ // 2
        piece = w2all.at[(y - d) % 4, m0:m1, row + side * half : row + (side + 1) * half, :]
        return remote(piece, piece, w_s.at[part, 1, side], w_r.at[part, 1, side], y_peer(d))

    def w_send(part):
        for d in (1, -1):
            w_copy(part, d).start()

    def w_pass(part):
        for d in (1, -1):
            w_copy(part, d).wait_recv()
            w_forward(part, d).start()

    def w_land(part):
        for d in (1, -1):
            w_forward(part, d).wait_recv()

    w_local = pltpu.make_async_copy(w2, w2all.at[y], wl_s)
    w_local.start()
    w_send(0)

    for zb in range(2):
        rows = rows_of(xl, z)
        piece = ebuf.at[k, rows, pl.ds(zb * C, C)]
        remote(piece, piece, sc_s.at[zb], sc_r.at[zb], core_sib).wait_recv()

    def az_copy(d):
        piece = ebuf.at[k, rows_of(xl, z), :]
        return remote(piece, piece, az_s.at[d], az_r.at[d], z_peer(d))

    def ax_copy(d):
        piece = ebuf.at[k, rows_of(xl, (z - d) % 8), :]
        return remote(piece, piece, ax_s.at[d], ax_r.at[d], x_sib)

    def ac_copy(d, s):
        xl_ = (xl + s) % 2
        piece = ebuf.at[k, rows_of(xl_, (z - d) % 8), :]
        return remote(piece, piece, ac_s.at[s, d], ac_r.at[s, d], core_sib)

    order = (1, 7, 2, 6, 3, 5, 4)
    for d in order:
        az_copy(d).start()
    ax_copy(0).start()
    ac_copy(0, 0).start()
    for d in order:
        az_copy(d).wait_recv()
        ax_copy(d).start()
        ac_copy(d, 0).start()
    for d in (0,) + order:
        ax_copy(d).wait_recv()
        ac_copy(d, 1).start()
    for d in (0,) + order:
        ac_copy(d, 0).wait_recv()
        ac_copy(d, 1).wait_recv()

    gain = g1[pl.ds(pl.multiple_of(c * KD, KD), KD)].reshape(1, KD)
    squares = jnp.zeros((V, 1), F32)
    for q in range(4):
        e = ebuf[q % 2, :, (q // 2) * C : (q // 2 + 1) * C].astype(F32)
        squares = squares + jnp.sum(e * e, axis=1, keepdims=True)
        xbuf[:, q * C : (q + 1) * C] = (e * gain[:, q * C : (q + 1) * C]).astype(BF16)
    psq[...] = jnp.transpose(jnp.broadcast_to(squares, (V, 128)))[0:1, :]

    mine = pl.ds(pl.multiple_of(c * 64, 64), 64)

    def rs_copy(kind, d):
        rows = pl.ds(pl.multiple_of(((c + d) % 8) * 64, 64), 64)
        src = (pkv.at[rows, :], pq.at[rows, :], psq)[kind]
        dst = (rskv, rsq, rssq)[kind].at[d - 1]
        return remote(src, dst, rs_s.at[kind, d - 1], rs_r.at[kind, d - 1], ctx_peer(d))

    def ag_copy(kind, d):
        piece = (tkv, tq)[kind].at[mine, :]
        return remote(piece, piece, ag_s.at[kind, d - 1], ag_r.at[kind, d - 1], ctx_peer(d))

    ctx_order = (4, 1, 7, 2, 6, 3, 5)
    for d in ctx_order:
        rs_copy(2, d).start()
    for m in (1, 2):
        pkv[:, (m - 1) * C : m * C] = dot(xbuf[...], w1[m]).astype(BF16)
    for d in ctx_order:
        rs_copy(0, d).start()
    pq[...] = dot(xbuf[...], w1[0]).astype(BF16)
    for d in ctx_order:
        rs_copy(1, d).start()

    sq = psq[...]
    for d in ctx_order:
        rs_copy(2, d).wait_recv()
        sq = sq + rssq[d - 1]
    row = lax.rsqrt(sq / D + EPS)
    ssb[0] = jnp.transpose(jnp.broadcast_to(row, (128, V)))
    scale_row = ssb[0, mine, :][:, 0:1]
    total = pkv[mine, :].astype(F32)
    for d in ctx_order:
        rs_copy(0, d).wait_recv()
        total = total + rskv[d - 1].astype(F32)
    tkv[mine, :] = (total * scale_row).astype(BF16)
    for d in ctx_order:
        ag_copy(0, d).start()
    total = pq[mine, :].astype(F32)
    for d in ctx_order:
        rs_copy(1, d).wait_recv()
        total = total + rsq[d - 1].astype(F32)
    tq[mine, :] = (total * scale_row).astype(BF16)
    for d in ctx_order:
        ag_copy(1, d).start()

    @pl.when(c > 0)
    def _():
        id_copy().wait_recv()

    @pl.when(c == 0)
    def _():
        idbuf[...] = jnp.full(idbuf.shape, -1, jnp.int32)

    for d in ctx_order:
        ag_copy(0, d).wait_recv()

    def one_hot(chunk):
        row = idbuf[128 + chunk * 128 : 256 + chunk * 128] if chunk < 2 else ids[(chunk - 2) * 128 : (chunk - 1) * 128]
        words = lax.broadcasted_iota(jnp.int32, (V, 128), 0)
        return jnp.where(words == row.reshape(1, 128), 1.0, 0.0).astype(BF16)

    def pick(hot, values):
        return lax.dot_general(hot, values, (((0,), (0,)), ((), ())), preferred_element_type=F32)

    for chunk in range(5):
        sbuf[chunk * 128 : (chunk + 1) * 128, C:] = pick(one_hot(chunk), tkv[...])

    def short(m, start, size, lanes=slice(0, C)):
        cols = slice(m * C + lanes.start, m * C + lanes.stop)
        out = sf[0, m : m + 1, lanes] * sbuf[start : start + size, cols]
        for j in range(1, 3):
            out = out + sf[j, m : m + 1, lanes] * sbuf[start - j : start - j + size, cols]
        return out

    for chunk in range(4):
        prod = (short(1, 128 + chunk * 128, 128) * short(2, 128 + chunk * 128, 128)).astype(BF16).astype(F32)
        for lt in range(2):
            prbuf[lt, chunk * 128 : (chunk + 1) * 128, :] = prod[:, lt * 128 : (lt + 1) * 128]

    def cols_of(z_, k_, h):
        return pl.ds(pl.multiple_of((z_ * 2 + k_) * C + h * 128, 128), 128)

    def e1_copy(a, h):
        dst = mall.at[xh, :, cols_of(z, k, h)]
        src = mbuf.at[h]
        return src, dst, remote(src, dst, e1_s.at[a, h], e1_r.at[xh, h], dev(xl, y, a, z, k))

    def e1_send(h):
        for a in range(2):
            src, dst, cp = e1_copy(a, h)
            me = (xl == xh) & (xl == a)

            @pl.when(me)
            def _():
                pltpu.make_async_copy(src, dst, e1_r.at[xh, h]).start()

            @pl.when(jnp.logical_not(me))
            def _():
                cp.start()

    LANE_T = T // 8

    def convolve(lt):
        @pl.loop(0, LANE_T + LONG - 1)
        def _(i):
            ext[i] = prbuf[lt, pl.ds(i + 1, 8, stride=LANE_T), :]

        for ig in range(3):

            def taps(j8, acc):
                window = ext[pl.ds(ig * 16 + 120 - 8 * j8, 23)]
                coef = lf[pl.ds(pl.multiple_of(8 * j8, 8), 8), lt * 128 : (lt + 1) * 128]
                for jj in range(8):
                    acc = acc + coef[jj : jj + 1, :][None] * window[7 - jj : 23 - jj]
                return acc

            acc = lax.fori_loop(0, LONG // 8, taps, jnp.zeros((16, 8, 128), F32))
            for ii in range(16):
                lcbuf[pl.ds(ig * 16 + ii, 8, stride=LANE_T), :] = acc[ii]

    def residual(lt):
        lanes = slice(lt * 128, (lt + 1) * 128)
        for chunk in range(3):
            rows = slice(chunk * 128, (chunk + 1) * 128)
            features = pick(one_hot(chunk + 2), emb[:, lanes])
            gate = short(0, 256 + chunk * 128, 128, lanes)
            mixed = (features + gate * lcbuf[rows, :]).astype(BF16)
            mbuf[lt, rows, :] = mixed
            mixed_out[rows, lanes] = mixed

    convolve(0)
    for d in ctx_order:
        ag_copy(1, d).wait_recv()
    w_pass(0)
    w_send(1)
    for chunk in range(1, 5):
        sbuf[chunk * 128 : (chunk + 1) * 128, :C] = pick(one_hot(chunk), tq[...])
    residual(0)
    e1_send(0)
    convolve(1)
    residual(1)
    e1_send(1)

    def chunk_of(b, z_, k_, h):
        return mall.at[b, :, cols_of(z_, k_, h)]

    def zr_copy(b, s, h):
        piece = chunk_of(b, (z - s) % 8, k, h)
        return remote(piece, piece, zr_s.at[b, s, h], zr_r.at[b, s, h], z_peer(1))

    def zl_copy(b, s, h):
        piece = chunk_of(b, (z + s) % 8, k, h)
        return remote(piece, piece, zl_s.at[b, s, h], zl_r.at[b, s, h], z_peer(-1))

    def sib_copy(b, s, h):
        piece = chunk_of(b, (z + s) % 8, k, h)
        return remote(piece, piece, sib_s.at[b, s, h], sib_r.at[b, s, h], core_sib)

    def ring_start(b):
        for h in range(2):
            piece = chunk_of(b, z, k, h)
            remote(piece, piece, e1_s.at[0, h], e1_r.at[b, h], core_sib).wait_recv()
            zr_copy(b, 0, h).start()
            zl_copy(b, 0, h).start()
            sib_copy(b, 0, h).start()

    def ring_step(b, s):
        for h in range(2):
            if s < 4 or h == 0:
                zr_copy(b, s - 1, h).wait_recv()
                if s < 3 or (s == 3 and h == 0):
                    zr_copy(b, s, h).start()
                sib_copy(b, 8 - s, h).start()
            if s < 4 or h == 1:
                zl_copy(b, s - 1, h).wait_recv()
                if s < 3 or (s == 3 and h == 1):
                    zl_copy(b, s, h).start()
                sib_copy(b, s, h).start()

    def ring_end(b):
        for s in range(8):
            for h in range(2):
                sib_copy(b, s, h).wait_recv()

    def scale(b, ys):
        gain2 = g2[pl.ds(pl.multiple_of((4 * xh + ys) * KD, KD), KD)].reshape(1, KD)
        cols = pl.ds(pl.multiple_of(ys * KD, KD), KD)
        for r in range(3):
            rows = slice(r * 128, (r + 1) * 128)
            part = mall[b, rows, cols].astype(F32)
            squares_ = jnp.broadcast_to(jnp.sum(part * part, axis=1, keepdims=True), (128, 128))
            ssb[b, rows, :] = squares_ if ys == 0 else ssb[b, rows, :] + squares_
            xs[b, rows, cols] = (part * gain2).astype(BF16)

    def project(b, ys, ms):
        for m in ms:
            cols = slice(m * C, (m + 1) * C)
            term = dot(xs[b, :, ys * KD : (ys + 1) * KD], w2all[ys, m])
            pp[b, :, cols] = term if ys == 0 else pp[b, :, cols] + term

    def g_copy(b, m):
        if m == 3:
            return remote(sqs.at[b], sqr.at[b], g_s.at[b, m], g_r.at[b, m], x_far)
        return remote(gs.at[b, m], gr.at[b, m], g_s.at[b, m], g_r.at[b, m], x_far)

    def head_cols(m, h):
        return pl.ds(pl.multiple_of(m * C + h * HEAD, HEAD), HEAD)

    def send_half(b, ms):
        for m in ms:
            gs[b, m] = pp[b, :, head_cols(m, 1 - xh)].astype(BF16)
            g_copy(b, m).start()

    def send_squares(b):
        sqs[b] = jnp.transpose(ssb[b, :T, :])[0:1, :]
        g_copy(b, 3).start()

    def row_factor(b):
        g_copy(b, 3).wait_recv()
        other = jnp.transpose(jnp.broadcast_to(sqr[b], (128, T)))
        ssb[b, :T, :] = lax.rsqrt((ssb[b, :T, :] + other) / D + EPS)

    def head_norm(values):
        values = values.astype(F32)
        return (values * lax.rsqrt(jnp.mean(values * values, axis=1, keepdims=True) + EPS)).astype(BF16)

    def kv_copy(b, d):
        block = kvall.at[y, b]
        return remote(block, block, kv_s.at[b, d - 1], kv_r.at[b, d - 1], y_peer(d))

    def joined(b, m):
        g_copy(b, m).wait_recv()
        return ((pp[b, :, head_cols(m, xh)] + gr[b, m].astype(F32)) * ssb[b, :T, :]).astype(BF16)

    def finish_kv(b):
        row_factor(b)
        kvall[y, b, 0] = head_norm(joined(b, 1))
        kvall[y, b, 1] = joined(b, 2)
        for d in range(1, 4):
            kv_copy(b, d).start()

    def finish_q(b):
        qbuf[b] = head_norm(joined(b, 0))

    def kv_wait(b):
        for d in range(1, 4):
            kv_copy(b, d).wait_recv()

    ring_start(0)
    ring_step(0, 1)
    w_pass(1)
    w_send(2)
    ring_step(0, 2)
    ring_step(0, 3)
    ring_start(1)
    ring_step(0, 4)
    ring_end(0)
    w_local.wait()
    w_land(0)
    w_land(1)
    scale(0, 0)
    project(0, 0, (1, 2))
    ring_step(1, 1)
    scale(0, 1)
    project(0, 1, (1, 2))
    scale(0, 2)
    project(0, 2, (1, 2))
    ring_step(1, 2)
    scale(0, 3)
    project(0, 3, (1, 2))
    send_squares(0)
    send_half(0, (1, 2))
    w_pass(2)
    ring_step(1, 3)
    finish_kv(0)
    ring_step(1, 4)
    ring_end(1)
    for ys in range(4):
        scale(1, ys)
        project(1, ys, (1, 2))
    send_squares(1)
    send_half(1, (1, 2))
    w_land(2)
    for b in range(2):
        for ys in range(4):
            project(b, ys, (0,))
        send_half(b, (0,))
    finish_kv(1)
    finish_q(0)
    finish_q(1)
    kv_wait(0)

    factor = 2.0 * HEAD ** -0.5

    def attend(b):
        @pl.loop(0, 3)
        def _(qc):
            rows = pl.ds(pl.multiple_of(qc * 128, 128), 128)
            query = qbuf[b, rows, :]

            def weights(ys, kb):
                score = lax.dot_general(
                    query, kvall[ys, kb, 0], (((1,), (1,)), ((), ())), preferred_element_type=F32
                )
                return jnp.exp(score * factor)

            def add(carry, weight, ys, kb):
                num, den = carry
                den = den + jnp.sum(weight, axis=1, keepdims=True)
                return num + dot(weight.astype(BF16), kvall[ys, kb, 1]), den

            def full(kb):
                return lambda ys, carry: add(carry, weights(ys, kb), ys, kb)

            carry = (jnp.zeros((128, HEAD), F32), jnp.zeros((128, 1), F32))
            if b == 1:
                carry = lax.fori_loop(0, 4, full(0), carry)
            carry = lax.fori_loop(0, y, full(b), carry)
            weight = weights(y, b)
            at = qc * 128 + lax.broadcasted_iota(jnp.int32, (128, T), 0)
            key = lax.broadcasted_iota(jnp.int32, (128, T), 1)
            weight = jnp.where(key <= at, weight, 0.0)
            num, den = add(carry, weight, y, b)
            oloc[b, rows, :] = (num / den).astype(BF16)

    attend(0)
    kv_wait(1)
    attend(1)

    here = pl.ds(pl.multiple_of(xh * HEAD, HEAD), HEAD)
    there = pl.ds(pl.multiple_of((1 - xh) * HEAD, HEAD), HEAD)
    o_copy = remote(oloc.at[1 - xh], obuf, o_s, o_r, x_far)
    o_copy.start()
    att_out[:, here] = oloc[xh]
    o_copy.wait_recv()
    att_out[:, there] = obuf[...]

    @pl.when(c < 7)
    def _():
        id_copy().wait_send()

    for e in range(2):
        me = (xl == xh) & (z // 2 == y) & (2 * y + e == z)

        @pl.when(jnp.logical_not(me))
        def _():
            sc_copy(e)[2].wait_send()

    for a in range(2):
        me = (xl == xh) & (xl == a)

        @pl.when(jnp.logical_not(me))
        def _():
            for h in range(2):
                e1_copy(a, h)[2].wait_send()

    for part in range(3):
        for d in (1, -1):
            w_copy(part, d).wait_send()
            w_forward(part, d).wait_send()
    for d in order:
        az_copy(d).wait_send()
    for d in range(8):
        ax_copy(d).wait_send()
        ac_copy(d, 0).wait_send()
        ac_copy(d, 1).wait_send()
    for d in range(1, 8):
        for kind in range(3):
            rs_copy(kind, d).wait_send()
        for kind in range(2):
            ag_copy(kind, d).wait_send()
    for b in range(2):
        for s in range(4):
            for h in range(2):
                if s < 3 or h == 0:
                    zr_copy(b, s, h).wait_send()
                if s < 3 or h == 1:
                    zl_copy(b, s, h).wait_send()
        for s in range(8):
            for h in range(2):
                sib_copy(b, s, h).wait_send()
        for m in range(4):
            g_copy(b, m).wait_send()
        for d in range(1, 4):
            kv_copy(b, d).wait_send()
    o_copy.wait_send()


def local(base_ids, embedding, first_gain, hyena_weight, short_filter, long_filter, second_gain, attn_weight):
    dma = pltpu.SemaphoreType.DMA
    vmem = pltpu.VMEM
    scratch = [
        vmem((T,), jnp.int32),
        vmem((2, V, 2 * C), BF16),
        vmem((V, KD), BF16),
        vmem((V, 2 * C), BF16),
        vmem((V, C), BF16),
        vmem((1, V), F32),
        vmem((7, 64, 2 * C), BF16),
        vmem((7, 64, C), BF16),
        vmem((7, 1, V), F32),
        vmem((V, 2 * C), BF16),
        vmem((V, C), BF16),
        vmem((640, 3 * C), F32),
        vmem((2, 512, 128), F32),
        vmem((T // 8 + LONG, 8, 128), F32),
        vmem((T, 128), F32),
        vmem((2, T, 128), BF16),
        vmem((4, 3, KD, C), BF16),
        vmem((2, T, 16 * C), BF16),
        vmem((2, T, 16 * C), BF16),
        vmem((2, T, 3 * C), F32),
        vmem((2, V, 128), F32),
        vmem((2, 3, T, HEAD), BF16),
        vmem((2, 3, T, HEAD), BF16),
        vmem((2, 1, T), F32),
        vmem((2, 1, T), F32),
        vmem((2, T, HEAD), BF16),
        vmem((4, 2, 2, T, HEAD), BF16),
        vmem((2, T, HEAD), BF16),
        vmem((T, HEAD), BF16),
        dma, dma,
        dma((2,)), dma((2,)),
        dma((8,)), dma((8,)),
        dma((8,)), dma((8,)),
        dma((2, 8)), dma((2, 8)),
        dma((3, 7)), dma((3, 7)),
        dma((2, 7)), dma((2, 7)),
        dma((3, 2, 2)), dma((3, 2, 2)), dma,
        dma((2, 2)), dma((2, 2)),
        dma((2, 4, 2)), dma((2, 4, 2)),
        dma((2, 4, 2)), dma((2, 4, 2)),
        dma((2, 8, 2)), dma((2, 8, 2)),
        dma((2, 4)), dma((2, 4)),
        dma((2, 3)), dma((2, 3)),
        dma, dma,
    ]
    return pl.pallas_call(
        kernel,
        out_shape=(jax.ShapeDtypeStruct((T, C), BF16), jax.ShapeDtypeStruct((T, C), BF16)),
        in_specs=[pl.BlockSpec(memory_space=pltpu.VMEM)] * 8,
        out_specs=(pl.BlockSpec(memory_space=pltpu.VMEM), pl.BlockSpec(memory_space=pltpu.VMEM)),
        scratch_shapes=scratch,
        compiler_params=pltpu.CompilerParams(
            collective_id=0, has_side_effects=True, vmem_limit_bytes=56 << 20
        ),
    )(
        base_ids,
        embedding,
        first_gain,
        jnp.transpose(hyena_weight, (1, 0, 2)),
        short_filter,
        long_filter,
        second_gain,
        jnp.transpose(attn_weight, (1, 0, 2)),
    )


def solution(mesh):
    return jax.shard_map(
        local,
        mesh=mesh,
        in_specs=(
            P("ctx"),
            P(None, "fsdp"),
            P(),
            P("ctx", None, "fsdp"),
            P(None, None, "fsdp"),
            P(None, "fsdp"),
            P(),
            P("ctx", None, "fsdp"),
        ),
        out_specs=(P("ctx", "fsdp"), P("ctx", "fsdp")),
        check_vma=False,
    )
```

```python
import math

import jax
import jax.numpy as jnp
from jax import lax
from jax.experimental import pallas as pl
from jax.experimental.pallas import tpu as pltpu
from jax.sharding import PartitionSpec as P

MESH = pl.DeviceIdType.MESH
F32, BF16 = jnp.float32, jnp.bfloat16
T = 384
V = 512
C = 256
KD = 1024
D = 8192
HEAD = 128
LONG = 128
EPS = 1e-6


def dot(a, b):
    return jnp.dot(a, b, preferred_element_type=F32)


def kernel(
    ids, emb, g1, w1, sf, lf, g2, w2,
    mixed_out, att_out,
    idbuf, ebuf, xbuf, pkv, pq, psq, rskv, rsq, rssq, tkv, tq, sbuf, prbuf, taps, coef, xo, xu, xsum, dv, lcbuf, mbuf,
    w2all, mall, xs, pp, ssb, gs, gr, sqs, sqr, qbuf, kvall, num, den, oloc, obuf,
    id_s, id_r, sc_s, sc_r, az_s, az_r, ax_s, ax_r, ac_s, ac_r,
    rs_s, rs_r, ag_s, ag_r, w_s, w_r, wl_s, e1_s, e1_r, zr_s, zr_r, zl_s, zl_r, sw_s, sw_r, sib_s, sib_r,
    g_s, g_r, kv_s, kv_r, o_s, o_r,
):
    c = lax.axis_index("ctx")
    f = lax.axis_index("fsdp")
    xh, y = c // 4, c % 4
    xl, z, k = f // 16, (f // 2) % 8, f % 2

    def dev(xh_, y_, xl_, z_, k_):
        return (xh_ * 4 + y_, xl_ * 16 + z_ * 2 + k_)

    def ctx_peer(d):
        return ((c + d) % 8, f)

    def z_peer(d):
        return dev(xh, y, xl, (z + d) % 8, k)

    def y_peer(d):
        return dev(xh, (y + d) % 4, xl, z, k)

    x_sib = dev(xh, y, 1 - xl, z, k)
    core_sib = dev(xh, y, xl, z, 1 - k)
    x_far = dev(1 - xh, y, xl, z, k)

    def remote(src, dst, ss, rs, to):
        return pltpu.make_async_remote_copy(
            src_ref=src, dst_ref=dst, send_sem=ss, recv_sem=rs, device_id=to, device_id_type=MESH
        )

    barrier = pltpu.get_barrier_semaphore()
    count = 0
    peers = [ctx_peer(d) for d in range(1, 8)] + [z_peer(d) for d in range(1, 8)] + [x_sib, core_sib]
    peers += [dev(xl, z // 2, xh, 2 * ((y + 4 - z // 2) % 4) + e, k) for e in range(2)]
    peers += [dev(xl, (y + z // 2) % 4, xh, 2 * y + e, k) for e in range(2)]
    peers += [dev(xl, y, a, z, k) for a in range(2)]
    peers += [dev(a, y, xh, z, k) for a in range(2)]
    for p in peers:
        pl.semaphore_signal(barrier, inc=1, device_id=p, device_id_type=MESH)
        count += 1
    pl.semaphore_wait(barrier, count)

    def id_copy():
        return remote(ids, idbuf, id_s, id_r, ctx_peer(1))

    @pl.when(c < 7)
    def _():
        id_copy().start()

    rows_of = lambda xl_, z_: pl.ds(pl.multiple_of(xl_ * 256 + z_ * 32, 32), 32)

    def sc_copy(e):
        to_z = 2 * ((y + 4 - z // 2) % 4) + e
        rows = rows_of(xh, to_z)
        cols = pl.ds(pl.multiple_of((z % 2) * C, C), C)
        src, dst = emb.at[rows, :], ebuf.at[k, rows, cols]
        same = (xl == xh) & (z // 2 == y) & (to_z == z)
        return same, src, dst, remote(src, dst, sc_s.at[e], sc_r.at[z % 2], dev(xl, z // 2, xh, to_z, k))

    for e in range(2):
        same, src, dst, cp = sc_copy(e)

        @pl.when(same)
        def _():
            pltpu.make_async_copy(src, dst, sc_r.at[z % 2]).start()

        @pl.when(jnp.logical_not(same))
        def _():
            cp.start()

    W_PARTS = ((1, 3, 0, 640), (1, 3, 640, KD - 640), (0, 1, 0, KD))

    def w_copy(part, d):
        m0, m1, row, count_ = W_PARTS[part]
        side = {1: 0, -1: 1}[d]
        cut = (slice(m0, m1), slice(row, row + count_), slice(None))
        return remote(
            w2.at[cut], w2all.at[cut[0], y, cut[1]], w_s.at[part, 0, side], w_r.at[part, 0, side], y_peer(d)
        )

    def w_forward(part, d):
        m0, m1, row, count_ = W_PARTS[part]
        side = {1: 0, -1: 1}[d]
        half = count_ // 2
        piece = w2all.at[m0:m1, (y - d) % 4, row + side * half : row + (side + 1) * half, :]
        return remote(piece, piece, w_s.at[part, 1, side], w_r.at[part, 1, side], y_peer(d))

    def w_send(part):
        for d in (1, -1):
            w_copy(part, d).start()

    def w_pass(part):
        for d in (1, -1):
            w_copy(part, d).wait_recv()
            w_forward(part, d).start()

    def w_land(part):
        for d in (1, -1):
            w_forward(part, d).wait_recv()

    w_local = pltpu.make_async_copy(w2, w2all.at[:, y], wl_s)
    w_local.start()
    w_send(0)

    def taps_of(lt):
        taps[...] = lf[:, lt * 128 : (lt + 1) * 128]
        even, odd = taps[pl.ds(0, LONG // 2, stride=2), :], taps[pl.ds(1, LONG // 2, stride=2), :]
        coef[lt, 0] = even
        coef[lt, 1] = odd
        coef[lt, 2] = even + odd

    taps_of(0)
    taps_of(1)

    for zb in range(2):
        rows = rows_of(xl, z)
        piece = ebuf.at[k, rows, pl.ds(zb * C, C)]
        remote(piece, piece, sc_s.at[zb], sc_r.at[zb], core_sib).wait_recv()

    def az_copy(d):
        piece = ebuf.at[k, rows_of(xl, z), :]
        return remote(piece, piece, az_s.at[d], az_r.at[d], z_peer(d))

    def ax_copy(d):
        piece = ebuf.at[k, rows_of(xl, (z - d) % 8), :]
        return remote(piece, piece, ax_s.at[d], ax_r.at[d], x_sib)

    def ac_copy(d, s):
        xl_ = (xl + s) % 2
        piece = ebuf.at[k, rows_of(xl_, (z - d) % 8), :]
        return remote(piece, piece, ac_s.at[s, d], ac_r.at[s, d], core_sib)

    order = (1, 7, 2, 6, 3, 5, 4)
    for d in order:
        az_copy(d).start()
    ax_copy(0).start()
    ac_copy(0, 0).start()
    for d in order:
        az_copy(d).wait_recv()
        ax_copy(d).start()
        ac_copy(d, 0).start()
    gain = g1[pl.ds(pl.multiple_of(c * KD, KD), KD)].reshape(1, KD)
    mine = pl.ds(pl.multiple_of(c * 64, 64), 64)

    def half_rows(hv):
        return pl.ds(pl.multiple_of(((xl + hv) % 2) * 256, 256), 256)

    def table(hv):
        rows = half_rows(hv)
        squares = jnp.zeros((256, 1), F32)
        for q in range(4):
            e = ebuf[q % 2, rows, (q // 2) * C : (q // 2 + 1) * C].astype(F32)
            squares = squares + jnp.sum(e * e, axis=1, keepdims=True)
            xbuf[:, q * C : (q + 1) * C] = (e * gain[:, q * C : (q + 1) * C]).astype(BF16)
        psq[hv] = jnp.transpose(jnp.broadcast_to(squares, (256, 128)))[0:1, :]
        terms = [dot(xbuf[...], w1[m]).astype(BF16) for m in (1, 2, 0)]
        pkv[rows, :C] = terms[0]
        pkv[rows, C:] = terms[1]
        pq[rows, :] = terms[2]

    def rs_copy(kind, hv, dy):
        half = (xl + hv) % 2
        to = half * 4 + (y + dy) % 4
        rows = pl.ds(pl.multiple_of(to * 64, 64), 64)
        src = (pkv.at[rows, :], pq.at[rows, :], psq.at[hv])[kind]
        dst = (rskv, rsq, rssq)[kind].at[c]
        return remote(src, dst, rs_s.at[kind, hv, dy], rs_r.at[kind, c], (to, f))

    def rs_each(hv, kinds, act):
        for kind in kinds:
            for dy in (2, 1, 3):
                act(rs_copy(kind, hv, dy))

            @pl.when((xl + hv) % 2 != xh)
            def _():
                act(rs_copy(kind, hv, 0))

    def rs_land(kind):
        slots = []
        for dx in (0, 1):
            for dy in (0, 1, 2, 3):
                if (dx, dy) != (0, 0):
                    slot = ((xh + dx) % 2) * 4 + (y + dy) % 4
                    src = (pkv.at[mine, :], pq.at[mine, :], psq.at[0])[kind]
                    dst = (rskv, rsq, rssq)[kind].at[slot]
                    remote(src, dst, rs_s.at[kind, 0, 0], rs_r.at[kind, slot], core_sib).wait_recv()
                    slots.append(slot)
        return slots

    def ag_copy(kind, d):
        piece = (tkv, tq)[kind].at[mine, :]
        return remote(piece, piece, ag_s.at[kind, d - 1], ag_r.at[kind, d - 1], ctx_peer(d))

    ctx_order = (4, 1, 7, 2, 6, 3, 5)
    for d in (0,) + order:
        ac_copy(d, 0).wait_recv()
    table(0)
    rs_each(0, (2, 0, 1), lambda copy: copy.start())
    for d in (0,) + order:
        ax_copy(d).wait_recv()
        ac_copy(d, 1).start()
    for d in (0,) + order:
        ac_copy(d, 1).wait_recv()
    table(1)
    rs_each(1, (2, 0, 1), lambda copy: copy.start())
    sq = psq[(xl + xh) % 2]
    for slot in rs_land(2):
        sq = sq + rssq[slot]
    row = lax.rsqrt(sq / D + EPS)
    ssb[0, :256, :] = jnp.transpose(jnp.broadcast_to(row, (128, 256)))
    scale_row = ssb[0, pl.ds(pl.multiple_of(y * 64, 64), 64), :][:, 0:1]
    total = pkv[mine, :].astype(F32)
    for slot in rs_land(0):
        total = total + rskv[slot].astype(F32)
    tkv[mine, :] = (total * scale_row).astype(BF16)
    for d in ctx_order:
        ag_copy(0, d).start()
    total = pq[mine, :].astype(F32)
    for slot in rs_land(1):
        total = total + rsq[slot].astype(F32)
    tq[mine, :] = (total * scale_row).astype(BF16)
    for d in ctx_order:
        ag_copy(1, d).start()

    @pl.when(c > 0)
    def _():
        id_copy().wait_recv()

    @pl.when(c == 0)
    def _():
        idbuf[...] = jnp.full(idbuf.shape, -1, jnp.int32)

    for d in ctx_order:
        ag_copy(0, d).wait_recv()

    w_pass(0)
    w_send(1)
    def one_hot(chunk):
        row = idbuf[128 + chunk * 128 : 256 + chunk * 128] if chunk < 2 else ids[(chunk - 2) * 128 : (chunk - 1) * 128]
        words = lax.broadcasted_iota(jnp.int32, (V, 128), 0)
        return jnp.where(words == row.reshape(1, 128), 1.0, 0.0).astype(BF16)

    def pick(hot, values):
        return lax.dot_general(hot, values, (((0,), (0,)), ((), ())), preferred_element_type=F32)

    for chunk in range(5):
        sbuf[chunk * 128 : (chunk + 1) * 128, C:] = pick(one_hot(chunk), tkv[...])

    def short(m, start, size, lanes=slice(0, C)):
        cols = slice(m * C + lanes.start, m * C + lanes.stop)
        out = sf[0, m : m + 1, lanes] * sbuf[start : start + size, cols]
        for j in range(1, 3):
            out = out + sf[j, m : m + 1, lanes] * sbuf[start - j : start - j + size, cols]
        return out

    for chunk in range(4):
        prod = (short(1, 128 + chunk * 128, 128) * short(2, 128 + chunk * 128, 128)).astype(BF16).astype(F32)
        for lt in range(2):
            prbuf[lt, chunk * 128 : (chunk + 1) * 128, :] = prod[:, lt * 128 : (lt + 1) * 128]

    def cols_of(z_, k_, h):
        return pl.ds(pl.multiple_of((z_ * 2 + k_) * C + h * 128, 128), 128)

    def rows_at(h, half):
        return pl.ds(0, T) if h == 0 else pl.ds(pl.multiple_of(half * (T // 2), T // 2), T // 2)

    def e1_copy(a, h):
        dst = mall.at[xh, rows_at(h, a), cols_of(z, k, h)]
        src = mbuf.at[h, rows_at(h, a), :]
        return src, dst, remote(src, dst, e1_s.at[a, h], e1_r.at[xh, h], dev(xl, y, a, z, k))

    def e1_send(h):
        for a in range(2):
            src, dst, cp = e1_copy(a, h)
            me = (xl == xh) & (xl == a)

            @pl.when(me)
            def _():
                pltpu.make_async_copy(src, dst, e1_r.at[xh, h]).start()

            @pl.when(jnp.logical_not(me))
            def _():
                cp.start()

    LANE_T = T // 8

    def half_filter(lt, which, src, start, count_):
        def eight(k8, acc):
            window = src[pl.ds(start + 56 - 8 * k8, count_ + 7)]
            row = coef[lt, which, pl.ds(pl.multiple_of(8 * k8, 8), 8), :]
            for jj in range(8):
                acc = acc + row[jj : jj + 1, :][None] * window[7 - jj : count_ + 7 - jj]
            return acc

        return lax.fori_loop(0, LONG // 16, eight, jnp.zeros((count_, 8, 128), F32), unroll=True)

    def convolve(lt):
        xu[0] = prbuf[lt, pl.ds(1, 8, stride=LANE_T), :]
        for m in range(87):
            odd = prbuf[lt, pl.ds(2 * m + 2, 8, stride=LANE_T), :]
            even = prbuf[lt, pl.ds(2 * m + 3, 8, stride=LANE_T), :]
            xo[m] = odd
            xu[m + 1] = even
            xsum[m] = odd + even
        dv[0:13] = half_filter(lt, 1, xu, 0, 13)
        dv[13:25] = half_filter(lt, 1, xu, 13, 12)
        for g in range(2):
            a = half_filter(lt, 0, xo, 12 * g, 12)
            t = half_filter(lt, 2, xsum, 12 * g, 12)
            for i in range(12):
                n = 12 * g + i
                lcbuf[pl.ds(2 * n, 8, stride=LANE_T), :] = a[i] + dv[n]
                lcbuf[pl.ds(2 * n + 1, 8, stride=LANE_T), :] = t[i] - a[i] - dv[n + 1]

    def residual(lt):
        lanes = slice(lt * 128, (lt + 1) * 128)
        for chunk in range(3):
            rows = slice(chunk * 128, (chunk + 1) * 128)
            features = pick(one_hot(chunk + 2), emb[:, lanes])
            gate = short(0, 256 + chunk * 128, 128, lanes)
            mixed = (features + gate * lcbuf[rows, :]).astype(BF16)
            mbuf[lt, rows, :] = mixed
            mixed_out[rows, lanes] = mixed

    convolve(0)
    for d in ctx_order:
        ag_copy(1, d).wait_recv()
    for chunk in range(1, 5):
        sbuf[chunk * 128 : (chunk + 1) * 128, :C] = pick(one_hot(chunk), tq[...])
    residual(0)
    e1_send(0)
    convolve(1)
    residual(1)
    e1_send(1)

    def chunk_of(b, z_, p):
        rows = rows_at(1, xl) if p == 2 else pl.ds(p * (T // 2), T // 2)
        return mall.at[b, rows, cols_of(z_, k, p // 2)]

    def zr_copy(b, s, p):
        piece = chunk_of(b, (z + 8 - s) % 8, p)
        return remote(piece, piece, zr_s.at[b, s, p], zr_r.at[b, s, p], z_peer(1))

    def zl_copy(b, s, p):
        piece = chunk_of(b, (z + s) % 8, p)
        return remote(piece, piece, zl_s.at[b, s, p], zl_r.at[b, s, p], z_peer(-1))

    def sib_copy(b, s, h):
        piece = mall.at[b, rows_at(h, xl), cols_of((z + s) % 8, k, h)]
        return remote(piece, piece, sib_s.at[b, s, h], sib_r.at[b, s, h], core_sib)

    def swap_copy(b, s):
        piece = mall.at[b, rows_at(1, xl), cols_of((z + s) % 8, k, 1)]
        return remote(piece, piece, sw_s.at[b, s], sw_r.at[b, s], x_sib)

    def sib2_copy(b, s):
        piece = mall.at[b, rows_at(1, 1 - xl), cols_of((z + s) % 8, k, 1)]
        return remote(piece, piece, sib_s.at[b, s, 2], sib_r.at[b, s, 2], core_sib)

    def share(b, s, p):
        if p > 0:
            sib_copy(b, s, p - 1).start()
        if p == 2:
            swap_copy(b, s).start()

    def swap_land(b, s):
        swap_copy(b, s).wait_recv()
        sib2_copy(b, s).start()

    def ring_start(b, h):
        piece = mall.at[b, rows_at(h, xl), cols_of(z, k, h)]
        remote(piece, piece, e1_s.at[0, h], e1_r.at[b, h], core_sib).wait_recv()
        for p in ((0, 1), (2,))[h]:
            zr_copy(b, 0, p).start()
            zl_copy(b, 0, p).start()
        share(b, 0, h + 1)

    def goes_right(s, p):
        return s < 3 or (s == 3 and p < 2)

    def goes_left(s, p):
        return s < 3 or (s == 3 and p == 2)

    def ring_step(b, s):
        for p in range(3):
            if goes_right(s - 1, p):
                zr_copy(b, s - 1, p).wait_recv()
                if goes_right(s, p):
                    zr_copy(b, s, p).start()
            if goes_left(s - 1, p):
                zl_copy(b, s - 1, p).wait_recv()
                if goes_left(s, p):
                    zl_copy(b, s, p).start()
            if goes_right(s - 1, p):
                share(b, 8 - s, p)
            if goes_left(s - 1, p) and s < 4 or s == 4 and p == 2:
                share(b, s, p)
        if s == 2:
            swap_land(b, 0)
        if s > 2:
            swap_land(b, 8 - (s - 2))
            swap_land(b, s - 2)

    def ring_end(b):
        for s in (5, 3, 4):
            swap_land(b, s)
        for s in range(8):
            for h in range(2):
                sib_copy(b, s, h).wait_recv()
            sib2_copy(b, s).wait_recv()

    def scale(b, ys):
        gain2 = g2[pl.ds(pl.multiple_of((4 * xh + ys) * KD, KD), KD)].reshape(1, KD)
        cols = pl.ds(pl.multiple_of(ys * KD, KD), KD)
        for r in range(3):
            rows = slice(r * 128, (r + 1) * 128)
            part = mall[b, rows, cols].astype(F32)
            squares_ = jnp.broadcast_to(jnp.sum(part * part, axis=1, keepdims=True), (128, 128))
            ssb[b, rows, :] = squares_ if ys == 0 else ssb[b, rows, :] + squares_
            xs[b, rows, cols] = (part * gain2).astype(BF16)

    def project(pairs):
        terms = [dot(xs[b], w2all[m].reshape(4 * KD, C)) for b, m in pairs]
        for (b, m), term in zip(pairs, terms):
            pp[b, :, m * C : (m + 1) * C] = term

    def g_copy(b, m):
        if m == 3:
            return remote(sqs.at[b], sqr.at[b], g_s.at[b, m], g_r.at[b, m], x_far)
        return remote(gs.at[b, m], gr.at[b, m], g_s.at[b, m], g_r.at[b, m], x_far)

    def head_cols(m, h):
        return pl.ds(pl.multiple_of(m * C + h * HEAD, HEAD), HEAD)

    def send_half(b, ms):
        for m in ms:
            gs[b, m] = pp[b, :, head_cols(m, 1 - xh)].astype(BF16)
            g_copy(b, m).start()

    def send_squares(b):
        sqs[b] = jnp.transpose(ssb[b, :T, :])[0:1, :]
        g_copy(b, 3).start()

    def row_factor(b):
        g_copy(b, 3).wait_recv()
        other = jnp.transpose(jnp.broadcast_to(sqr[b], (128, T)))
        ssb[b, :T, :] = lax.rsqrt((ssb[b, :T, :] + other) / D + EPS)

    def head_norm(values):
        values = values.astype(F32)
        return (values * lax.rsqrt(jnp.mean(values * values, axis=1, keepdims=True) + EPS)).astype(BF16)

    def kv_copy(b, d):
        block = kvall.at[y, b]
        side = {1: 0, -1: 1}[d]
        return remote(block, block, kv_s.at[b, side], kv_r.at[b, side], y_peer(d))

    def kv_forward(b, d):
        side = {1: 0, -1: 1}[d]
        part = kvall.at[(y + 4 - d) % 4, b, side]
        return remote(part, part, kv_s.at[b, 2 + side], kv_r.at[b, 2 + side], y_peer(d))

    def kv_pass(b):
        for d in (1, -1):
            kv_copy(b, d).wait_recv()
            kv_forward(b, d).start()

    def kv_land(b):
        for d in (1, -1):
            kv_forward(b, d).wait_recv()

    def joined(b, m):
        g_copy(b, m).wait_recv()
        return ((pp[b, :, head_cols(m, xh)] + gr[b, m].astype(F32)) * ssb[b, :T, :]).astype(BF16)

    def finish_kv(b):
        row_factor(b)
        kvall[y, b, 0] = head_norm(joined(b, 1))
        kvall[y, b, 1] = joined(b, 2)
        for d in (1, -1):
            kv_copy(b, d).start()

    def finish_q(b):
        qbuf[b] = head_norm(joined(b, 0))

    for h in range(2):
        for b in range(2):
            ring_start(b, h)
    ring_step(0, 1)
    ring_step(1, 1)
    ring_step(0, 2)
    w_pass(1)
    w_send(2)
    ring_step(1, 2)
    ring_step(0, 3)
    ring_step(1, 3)
    ring_step(0, 4)
    ring_step(1, 4)
    ring_end(0)
    for ys in range(4):
        scale(0, ys)
    send_squares(0)
    w_local.wait()
    w_land(0)
    w_land(1)
    project(((0, 1), (0, 2)))
    send_half(0, (1, 2))
    w_pass(2)
    ring_end(1)
    for ys in range(4):
        scale(1, ys)
    send_squares(1)
    project(((1, 1), (1, 2)))
    send_half(1, (1, 2))
    finish_kv(0)
    w_land(2)
    project(((0, 0), (1, 0)))
    send_half(0, (0,))
    send_half(1, (0,))
    kv_pass(0)
    finish_kv(1)
    finish_q(0)
    finish_q(1)
    kv_land(0)

    factor = 2.0 * HEAD ** -0.5 * math.log2(math.e)

    def key_block(b, ys, kb, diagonal=False, first=False):
        for qc in range(3):
            rows = slice(qc * 128, (qc + 1) * 128)
            width = (qc + 1) * 128 if diagonal else T
            score = lax.dot_general(
                qbuf[b, rows, :], kvall[ys, kb, 0, :width, :], (((1,), (1,)), ((), ())), preferred_element_type=F32
            )
            weight = jnp.exp2(score * factor)
            if diagonal:
                at = qc * 128 + lax.broadcasted_iota(jnp.int32, (128, width), 0)
                key = lax.broadcasted_iota(jnp.int32, (128, width), 1)
                weight = jnp.where(key <= at, weight, 0.0)
            part = weight[:, :128]
            for n in range(1, width // 128):
                part = part + weight[:, n * 128 : (n + 1) * 128]
            term = dot(weight.astype(BF16), kvall[ys, kb, 1, :width, :])
            if first:
                den[b, rows, :] = part
                num[b, rows, :] = term
            else:
                den[b, rows, :] += part
                num[b, rows, :] += term

    def earlier(b):
        @pl.loop(0, y)
        def _(ys):
            key_block(b, ys, b)

    def o_copy(b, chunk):
        rows = slice(chunk * 128, (chunk + 1) * 128)
        return remote(oloc.at[b, rows, :], obuf.at[rows, :], o_s.at[chunk], o_r.at[chunk], x_far)

    here = pl.ds(pl.multiple_of(xh * HEAD, HEAD), HEAD)
    there = pl.ds(pl.multiple_of((1 - xh) * HEAD, HEAD), HEAD)

    def conclude(b):
        for chunk in range(3):
            rows = slice(chunk * 128, (chunk + 1) * 128)
            out = num[b, rows, :] / jnp.sum(den[b, rows, :], axis=1, keepdims=True)
            oloc[b, rows, :] = out.astype(BF16)

            @pl.when(xh == 1 - b)
            def _():
                o_copy(b, chunk).start()

            @pl.when(xh == b)
            def _():
                att_out[rows, here] = oloc[b, rows, :]

    key_block(0, y, 0, diagonal=True, first=True)
    earlier(0)
    conclude(0)
    kv_pass(1)
    key_block(1, 0, 0, first=True)

    @pl.loop(1, 4)
    def _(ys):
        key_block(1, ys, 0)

    kv_land(1)
    key_block(1, y, 1, diagonal=True)
    earlier(1)
    conclude(1)
    for chunk in range(3):
        o_copy(0, chunk).wait_recv()
    att_out[:, there] = obuf[...]

    @pl.when(c < 7)
    def _():
        id_copy().wait_send()

    for e in range(2):
        same, _, _, cp = sc_copy(e)

        @pl.when(jnp.logical_not(same))
        def _():
            cp.wait_send()

    for a in range(2):
        me = (xl == xh) & (xl == a)

        @pl.when(jnp.logical_not(me))
        def _():
            for h in range(2):
                e1_copy(a, h)[2].wait_send()

    for part in range(3):
        for d in (1, -1):
            w_copy(part, d).wait_send()
            w_forward(part, d).wait_send()
    for d in order:
        az_copy(d).wait_send()
    for d in range(8):
        ax_copy(d).wait_send()
        ac_copy(d, 0).wait_send()
        ac_copy(d, 1).wait_send()
    for d in range(1, 8):
        for kind in range(2):
            ag_copy(kind, d).wait_send()
    for hv in range(2):
        rs_each(hv, range(3), lambda copy: copy.wait_send())
    for b in range(2):
        for s in range(4):
            for p in range(3):
                if goes_right(s, p):
                    zr_copy(b, s, p).wait_send()
                if goes_left(s, p):
                    zl_copy(b, s, p).wait_send()
        for s in range(8):
            for h in range(2):
                sib_copy(b, s, h).wait_send()
            sib2_copy(b, s).wait_send()
            swap_copy(b, s).wait_send()
        for m in range(4):
            g_copy(b, m).wait_send()
        for d in (1, -1):
            kv_copy(b, d).wait_send()
            kv_forward(b, d).wait_send()
    for chunk in range(3):
        o_copy(0, chunk).wait_send()


def hand_over(mixed, att, mixed_out, att_out):
    mixed_out[...] = mixed[...]
    att_out[...] = att[...]


def local(base_ids, embedding, first_gain, hyena_weight, short_filter, long_filter, second_gain, attn_weight):
    dma = pltpu.SemaphoreType.DMA
    vmem = pltpu.VMEM
    scratch = [
        vmem((T,), jnp.int32),
        vmem((2, V, 2 * C), BF16),
        vmem((256, KD), BF16),
        vmem((V, 2 * C), BF16),
        vmem((V, C), BF16),
        vmem((2, 1, 256), F32),
        vmem((8, 64, 2 * C), BF16),
        vmem((8, 64, C), BF16),
        vmem((8, 1, 256), F32),
        vmem((V, 2 * C), BF16),
        vmem((V, C), BF16),
        vmem((640, 3 * C), F32),
        vmem((2, 512, 128), F32),
        vmem((LONG, 128), F32),
        vmem((2, 3, LONG // 2, 128), F32),
        vmem((88, 8, 128), F32),
        vmem((88, 8, 128), F32),
        vmem((88, 8, 128), F32),
        vmem((25, 8, 128), F32),
        vmem((T, 128), F32),
        vmem((2, T, 128), BF16),
        vmem((3, 4, KD, C), BF16),
        vmem((2, T, 16 * C), BF16),
        vmem((2, T, 16 * C), BF16),
        vmem((2, T, 3 * C), F32),
        vmem((2, V, 128), F32),
        vmem((2, 3, T, HEAD), BF16),
        vmem((2, 3, T, HEAD), BF16),
        vmem((2, 1, T), F32),
        vmem((2, 1, T), F32),
        vmem((2, T, HEAD), BF16),
        vmem((4, 2, 2, T, HEAD), BF16),
        vmem((2, T, HEAD), F32),
        vmem((2, T, HEAD), F32),
        vmem((2, T, HEAD), BF16),
        vmem((T, HEAD), BF16),
        dma, dma,
        dma((2,)), dma((2,)),
        dma((8,)), dma((8,)),
        dma((8,)), dma((8,)),
        dma((2, 8)), dma((2, 8)),
        dma((3, 2, 4)), dma((3, 8)),
        dma((2, 7)), dma((2, 7)),
        dma((3, 2, 2)), dma((3, 2, 2)), dma,
        dma((2, 2)), dma((2, 2)),
        dma((2, 4, 3)), dma((2, 4, 3)),
        dma((2, 4, 3)), dma((2, 4, 3)),
        dma((2, 8)), dma((2, 8)),
        dma((2, 8, 3)), dma((2, 8, 3)),
        dma((2, 4)), dma((2, 4)),
        dma((2, 4)), dma((2, 4)),
        dma((3,)), dma((3,)),
    ]
    results = pl.pallas_call(
        kernel,
        out_shape=(jax.ShapeDtypeStruct((T, C), BF16), jax.ShapeDtypeStruct((T, C), BF16)),
        in_specs=[pl.BlockSpec(memory_space=pltpu.VMEM)] * 8,
        out_specs=(pl.BlockSpec(memory_space=pltpu.VMEM), pl.BlockSpec(memory_space=pltpu.VMEM)),
        scratch_shapes=scratch,
        compiler_params=pltpu.CompilerParams(
            collective_id=0, has_side_effects=True, vmem_limit_bytes=56 << 20
        ),
    )(
        base_ids,
        embedding,
        first_gain,
        jnp.transpose(hyena_weight, (1, 0, 2)),
        short_filter,
        long_filter,
        second_gain,
        jnp.transpose(attn_weight, (1, 0, 2)),
    )
    shape = jax.ShapeDtypeStruct((T, C), BF16)
    return pl.pallas_call(hand_over, out_shape=(shape, shape))(*results)


def solution(mesh):
    return jax.shard_map(
        local,
        mesh=mesh,
        in_specs=(
            P("ctx"),
            P(None, "fsdp"),
            P(),
            P("ctx", None, "fsdp"),
            P(None, None, "fsdp"),
            P(None, "fsdp"),
            P(),
            P("ctx", None, "fsdp"),
        ),
        out_specs=(P("ctx", "fsdp"), P("ctx", "fsdp")),
        check_vma=False,
    )
```

```python
import math

import jax
import jax.numpy as jnp
from jax import lax
from jax.experimental import pallas as pl
from jax.experimental.pallas import tpu as pltpu
from jax.sharding import PartitionSpec as P

MESH = pl.DeviceIdType.MESH
F32, BF16 = jnp.float32, jnp.bfloat16
T = 384
V = 512
C = 256
KD = 1024
D = 8192
HEAD = 128
LONG = 128
EPS = 1e-6


def dot(a, b):
    return jnp.dot(a, b, preferred_element_type=F32)


def kernel(
    ids, emb, g1, w1, sf, lf, g2, w2,
    mixed_out, att_out,
    idbuf, ebuf, xbuf, pkv, pq, psq, rskv, rsq, rssq, tkv, tq, sbuf, prbuf, taps, coef, xo, xu, xsum, dv, lcbuf, mbuf,
    w2all, mall, xs, pp, ssb, gs, gr, sqs, sqr, qbuf, kvall, num, den, oloc, obuf,
    id_s, id_r, sc_s, sc_r, az_s, az_r, ax_s, ax_r, ac_s, ac_r,
    rs_s, rs_r, ag_s, ag_r, w_s, w_r, wl_s, e1_s, e1_r, zr_s, zr_r, zl_s, zl_r, sw_s, sw_r, sib_s, sib_r,
    g_s, g_r, kv_s, kv_r, o_s, o_r,
):
    c = lax.axis_index("ctx")
    f = lax.axis_index("fsdp")
    xh, y = c // 4, c % 4
    xl, z, k = f // 16, (f // 2) % 8, f % 2

    def dev(xh_, y_, xl_, z_, k_):
        return (xh_ * 4 + y_, xl_ * 16 + z_ * 2 + k_)

    def ctx_peer(d):
        return ((c + d) % 8, f)

    def z_peer(d):
        return dev(xh, y, xl, (z + d) % 8, k)

    def y_peer(d):
        return dev(xh, (y + d) % 4, xl, z, k)

    x_sib = dev(xh, y, 1 - xl, z, k)
    core_sib = dev(xh, y, xl, z, 1 - k)
    x_far = dev(1 - xh, y, xl, z, k)

    def remote(src, dst, ss, rs, to):
        return pltpu.make_async_remote_copy(
            src_ref=src, dst_ref=dst, send_sem=ss, recv_sem=rs, device_id=to, device_id_type=MESH
        )

    barrier = pltpu.get_barrier_semaphore()
    count = 0
    peers = [ctx_peer(d) for d in range(1, 8)] + [z_peer(d) for d in (1, 7, 2, 6)] + [x_sib, core_sib]
    peers += [dev(xl, z // 2, xh, 2 * ((2 * (z // 2) + 6 - y) % 4) + e, k) for e in range(2)]
    peers += [dev(xl, (2 * y + 6 - z // 2) % 4, xh, 2 * y + e, k) for e in range(2)]
    peers += [dev(xl, y, a, z, k) for a in range(2)]
    peers += [dev(a, y, xh, z, k) for a in range(2)]
    for p in peers:
        pl.semaphore_signal(barrier, inc=1, device_id=p, device_id_type=MESH)
        count += 1
    pl.semaphore_wait(barrier, count)

    def id_copy():
        return remote(ids, idbuf, id_s, id_r, ctx_peer(1))

    @pl.when(c < 7)
    def _():
        id_copy().start()

    rows_of = lambda xl_, z_: pl.ds(pl.multiple_of(xl_ * 256 + (z_ % 4) * 64, 64), 64)

    def sc_copy(e):
        to_z = 2 * ((2 * (z // 2) + 6 - y) % 4) + e
        rows = rows_of(xh, to_z)
        cols = pl.ds(pl.multiple_of((z % 2) * C, C), C)
        src, dst = emb.at[rows, :], ebuf.at[k, rows, cols]
        same = (xl == xh) & (z // 2 == y) & (to_z == z)
        return same, src, dst, remote(src, dst, sc_s.at[e], sc_r.at[z % 2], dev(xl, z // 2, xh, to_z, k))

    for e in range(2):
        same, src, dst, cp = sc_copy(e)

        @pl.when(same)
        def _():
            pltpu.make_async_copy(src, dst, sc_r.at[z % 2]).start()

        @pl.when(jnp.logical_not(same))
        def _():
            cp.start()

    W_PARTS = ((1, 3, 0, 512), (1, 3, 512, KD - 512), (0, 1, 0, KD))

    def w_copy(part, d):
        m0, m1, row, count_ = W_PARTS[part]
        side = {1: 0, -1: 1}[d]
        cut = (slice(m0, m1), slice(row, row + count_), slice(None))
        return remote(
            w2.at[cut], w2all.at[cut[0], y, cut[1]], w_s.at[part, 0, side], w_r.at[part, 0, side], y_peer(d)
        )

    def w_forward(part, d):
        m0, m1, row, count_ = W_PARTS[part]
        side = {1: 0, -1: 1}[d]
        half = count_ // 2
        piece = w2all.at[m0:m1, (y - d) % 4, row + side * half : row + (side + 1) * half, :]
        return remote(piece, piece, w_s.at[part, 1, side], w_r.at[part, 1, side], y_peer(d))

    def w_send(part):
        for d in (1, -1):
            w_copy(part, d).start()

    def w_pass(part):
        for d in (1, -1):
            w_copy(part, d).wait_recv()
            w_forward(part, d).start()

    def w_land(part):
        for d in (1, -1):
            w_forward(part, d).wait_recv()

    w_local = pltpu.make_async_copy(w2, w2all.at[:, y], wl_s)
    w_local.start()
    w_send(0)

    def taps_of(lt):
        taps[...] = lf[:, lt * 128 : (lt + 1) * 128]
        even, odd = taps[pl.ds(0, LONG // 2, stride=2), :], taps[pl.ds(1, LONG // 2, stride=2), :]
        coef[lt, 0] = even
        coef[lt, 1] = odd
        coef[lt, 2] = even + odd

    taps_of(0)
    taps_of(1)

    for zb in range(2):
        rows = rows_of(xl, z)
        piece = ebuf.at[k, rows, pl.ds(zb * C, C)]
        remote(piece, piece, sc_s.at[zb], sc_r.at[zb], core_sib).wait_recv()

    def az_copy(d):
        piece = ebuf.at[k, rows_of(xl, z), :]
        return remote(piece, piece, az_s.at[d], az_r.at[d], z_peer(d))

    def ax_copy(d):
        piece = ebuf.at[k, rows_of(xl, (z - d) % 8), :]
        return remote(piece, piece, ax_s.at[d], ax_r.at[d], x_sib)

    def ac_copy(d, s):
        xl_ = (xl + s) % 2
        piece = ebuf.at[k, rows_of(xl_, (z - d) % 8), :]
        return remote(piece, piece, ac_s.at[s, d], ac_r.at[s, d], core_sib)

    order = (1, 7, 2)
    for d in order:
        az_copy(d).start()
    ax_copy(0).start()
    ac_copy(0, 0).start()
    for d in order:
        az_copy(d).wait_recv()
        ax_copy(d).start()
        ac_copy(d, 0).start()
    gain = g1[pl.ds(pl.multiple_of(c * KD, KD), KD)].reshape(1, KD)
    mine = pl.ds(pl.multiple_of(c * 64, 64), 64)

    def half_rows(hv):
        return pl.ds(pl.multiple_of(((xl + hv) % 2) * 256, 256), 256)

    def table(hv):
        rows = half_rows(hv)
        squares = jnp.zeros((256, 1), F32)
        for q in range(4):
            e = ebuf[q % 2, rows, (q // 2) * C : (q // 2 + 1) * C].astype(F32)
            squares = squares + jnp.sum(e * e, axis=1, keepdims=True)
            xbuf[:, q * C : (q + 1) * C] = (e * gain[:, q * C : (q + 1) * C]).astype(BF16)
        psq[hv] = jnp.transpose(jnp.broadcast_to(squares, (256, 128)))[0:1, :]
        terms = [dot(xbuf[...], w1[m]).astype(BF16) for m in (1, 2, 0)]
        pkv[rows, :C] = terms[0]
        pkv[rows, C:] = terms[1]
        pq[rows, :] = terms[2]

    def rs_copy(kind, hv, dy):
        half = (xl + hv) % 2
        to = half * 4 + (y + dy) % 4
        rows = pl.ds(pl.multiple_of(to * 64, 64), 64)
        src = (pkv.at[rows, :], pq.at[rows, :], psq.at[hv])[kind]
        dst = (rskv, rsq, rssq)[kind].at[c]
        return remote(src, dst, rs_s.at[kind, hv, dy], rs_r.at[kind, c], (to, f))

    def rs_each(hv, kinds, act):
        for kind in kinds:
            for dy in (2, 1, 3):
                act(rs_copy(kind, hv, dy))

            @pl.when((xl + hv) % 2 != xh)
            def _():
                act(rs_copy(kind, hv, 0))

    def rs_land(kind):
        slots = []
        for dx in (0, 1):
            for dy in (0, 1, 2, 3):
                if (dx, dy) != (0, 0):
                    slot = ((xh + dx) % 2) * 4 + (y + dy) % 4
                    src = (pkv.at[mine, :], pq.at[mine, :], psq.at[0])[kind]
                    dst = (rskv, rsq, rssq)[kind].at[slot]
                    remote(src, dst, rs_s.at[kind, 0, 0], rs_r.at[kind, slot], core_sib).wait_recv()
                    slots.append(slot)
        return slots

    def ag_copy(kind, d):
        piece = (tkv, tq)[kind].at[mine, :]
        return remote(piece, piece, ag_s.at[kind, d - 1], ag_r.at[kind, d - 1], ctx_peer(d))

    ctx_order = (4, 1, 7, 2, 6, 3, 5)
    for d in (0,) + order:
        ac_copy(d, 0).wait_recv()
    table(0)
    rs_each(0, (2, 0, 1), lambda copy: copy.start())
    for d in (0,) + order:
        ax_copy(d).wait_recv()
        ac_copy(d, 1).start()
    for d in (0,) + order:
        ac_copy(d, 1).wait_recv()
    table(1)
    rs_each(1, (2, 0, 1), lambda copy: copy.start())
    sq = psq[(xl + xh) % 2]
    for slot in rs_land(2):
        sq = sq + rssq[slot]
    row = lax.rsqrt(sq / D + EPS)
    ssb[0, :256, :] = jnp.transpose(jnp.broadcast_to(row, (128, 256)))
    scale_row = ssb[0, pl.ds(pl.multiple_of(y * 64, 64), 64), :][:, 0:1]
    total = pkv[mine, :].astype(F32)
    for slot in rs_land(0):
        total = total + rskv[slot].astype(F32)
    tkv[mine, :] = (total * scale_row).astype(BF16)
    for d in ctx_order:
        ag_copy(0, d).start()
    total = pq[mine, :].astype(F32)
    for slot in rs_land(1):
        total = total + rsq[slot].astype(F32)
    tq[mine, :] = (total * scale_row).astype(BF16)
    for d in ctx_order:
        ag_copy(1, d).start()

    @pl.when(c > 0)
    def _():
        id_copy().wait_recv()

    @pl.when(c == 0)
    def _():
        idbuf[...] = jnp.full(idbuf.shape, -1, jnp.int32)

    for d in ctx_order:
        ag_copy(0, d).wait_recv()

    w_pass(0)
    w_send(1)
    def one_hot(chunk):
        row = idbuf[128 + chunk * 128 : 256 + chunk * 128] if chunk < 2 else ids[(chunk - 2) * 128 : (chunk - 1) * 128]
        words = lax.broadcasted_iota(jnp.int32, (V, 128), 0)
        return jnp.where(words == row.reshape(1, 128), 1.0, 0.0).astype(BF16)

    def pick(hot, values):
        return lax.dot_general(hot, values, (((0,), (0,)), ((), ())), preferred_element_type=F32)

    for chunk in range(5):
        sbuf[chunk * 128 : (chunk + 1) * 128, C:] = pick(one_hot(chunk), tkv[...])

    def short(m, start, size, lanes=slice(0, C)):
        cols = slice(m * C + lanes.start, m * C + lanes.stop)
        out = sf[0, m : m + 1, lanes] * sbuf[start : start + size, cols]
        for j in range(1, 3):
            out = out + sf[j, m : m + 1, lanes] * sbuf[start - j : start - j + size, cols]
        return out

    for chunk in range(4):
        prod = (short(1, 128 + chunk * 128, 128) * short(2, 128 + chunk * 128, 128)).astype(BF16).astype(F32)
        for lt in range(2):
            prbuf[lt, chunk * 128 : (chunk + 1) * 128, :] = prod[:, lt * 128 : (lt + 1) * 128]

    def cols_of(z_, k_, h):
        return pl.ds(pl.multiple_of((z_ * 2 + k_) * C + h * 128, 128), 128)

    def rows_at(h, half):
        return pl.ds(0, T) if h == 0 else pl.ds(pl.multiple_of(half * (T // 2), T // 2), T // 2)

    def e1_copy(a, h):
        dst = mall.at[xh, rows_at(h, a), cols_of(z, k, h)]
        src = mbuf.at[h, rows_at(h, a), :]
        return src, dst, remote(src, dst, e1_s.at[a, h], e1_r.at[xh, h], dev(xl, y, a, z, k))

    def e1_send(h):
        for a in range(2):
            src, dst, cp = e1_copy(a, h)
            me = (xl == xh) & (xl == a)

            @pl.when(me)
            def _():
                pltpu.make_async_copy(src, dst, e1_r.at[xh, h]).start()

            @pl.when(jnp.logical_not(me))
            def _():
                cp.start()

    LANE_T = T // 8

    def half_filter(lt, which, src, start, count_):
        def eight(k8, acc):
            window = src[pl.ds(start + 56 - 8 * k8, count_ + 7)]
            row = coef[lt, which, pl.ds(pl.multiple_of(8 * k8, 8), 8), :]
            for jj in range(8):
                acc = acc + row[jj : jj + 1, :][None] * window[7 - jj : count_ + 7 - jj]
            return acc

        return lax.fori_loop(0, LONG // 16, eight, jnp.zeros((count_, 8, 128), F32), unroll=True)

    def convolve(lt):
        xu[0] = prbuf[lt, pl.ds(1, 8, stride=LANE_T), :]
        for m in range(87):
            odd = prbuf[lt, pl.ds(2 * m + 2, 8, stride=LANE_T), :]
            even = prbuf[lt, pl.ds(2 * m + 3, 8, stride=LANE_T), :]
            xo[m] = odd
            xu[m + 1] = even
            xsum[m] = odd + even
        dv[0:13] = half_filter(lt, 1, xu, 0, 13)
        dv[13:25] = half_filter(lt, 1, xu, 13, 12)
        for g in range(2):
            a = half_filter(lt, 0, xo, 12 * g, 12)
            t = half_filter(lt, 2, xsum, 12 * g, 12)
            for i in range(12):
                n = 12 * g + i
                lcbuf[pl.ds(2 * n, 8, stride=LANE_T), :] = a[i] + dv[n]
                lcbuf[pl.ds(2 * n + 1, 8, stride=LANE_T), :] = t[i] - a[i] - dv[n + 1]

    def residual(lt):
        lanes = slice(lt * 128, (lt + 1) * 128)
        for chunk in range(3):
            rows = slice(chunk * 128, (chunk + 1) * 128)
            features = pick(one_hot(chunk + 2), emb[:, lanes])
            gate = short(0, 256 + chunk * 128, 128, lanes)
            mixed = (features + gate * lcbuf[rows, :]).astype(BF16)
            mbuf[lt, rows, :] = mixed
            mixed_out[rows, lanes] = mixed

    convolve(0)
    for d in ctx_order:
        ag_copy(1, d).wait_recv()
    for chunk in range(1, 5):
        sbuf[chunk * 128 : (chunk + 1) * 128, :C] = pick(one_hot(chunk), tq[...])
    residual(0)
    e1_send(0)
    convolve(1)
    residual(1)
    e1_send(1)

    def chunk_of(b, z_, p):
        rows = rows_at(1, xl) if p == 2 else pl.ds(p * (T // 2), T // 2)
        return mall.at[b, rows, cols_of(z_, k, p // 2)]

    def zr_copy(b, s, p):
        piece = chunk_of(b, (z + 8 - s) % 8, p)
        return remote(piece, piece, zr_s.at[b, s, p], zr_r.at[b, s, p], z_peer(1))

    def zl_copy(b, s, p):
        piece = chunk_of(b, (z + s) % 8, p)
        return remote(piece, piece, zl_s.at[b, s, p], zl_r.at[b, s, p], z_peer(-1))

    def sib_copy(b, s, h):
        piece = mall.at[b, rows_at(h, xl), cols_of((z + s) % 8, k, h)]
        return remote(piece, piece, sib_s.at[b, s, h], sib_r.at[b, s, h], core_sib)

    def swap_copy(b, s):
        piece = mall.at[b, rows_at(1, xl), cols_of((z + s) % 8, k, 1)]
        return remote(piece, piece, sw_s.at[b, s], sw_r.at[b, s], x_sib)

    def sib2_copy(b, s):
        piece = mall.at[b, rows_at(1, 1 - xl), cols_of((z + s) % 8, k, 1)]
        return remote(piece, piece, sib_s.at[b, s, 2], sib_r.at[b, s, 2], core_sib)

    def share(b, s, p):
        if p > 0:
            sib_copy(b, s, p - 1).start()
        if p == 2:
            swap_copy(b, s).start()

    def swap_land(b, s):
        swap_copy(b, s).wait_recv()
        sib2_copy(b, s).start()

    def ring_start(b, h):
        piece = mall.at[b, rows_at(h, xl), cols_of(z, k, h)]
        remote(piece, piece, e1_s.at[0, h], e1_r.at[b, h], core_sib).wait_recv()
        for p in ((0, 1), (2,))[h]:
            zr_copy(b, 0, p).start()
            zl_copy(b, 0, p).start()
        share(b, 0, h + 1)

    def goes_right(s, p):
        return s < 3 or (s == 3 and p < 2)

    def goes_left(s, p):
        return s < 3 or (s == 3 and p == 2)

    def ring_step(b, s):
        for near in ((0,), (7, 1), (6, 2), (5, 3))[s - 1]:
            swap_land(b, near)
        for p in range(3):
            if goes_right(s - 1, p):
                zr_copy(b, s - 1, p).wait_recv()
                if goes_right(s, p):
                    zr_copy(b, s, p).start()
            if goes_left(s - 1, p):
                zl_copy(b, s - 1, p).wait_recv()
                if goes_left(s, p):
                    zl_copy(b, s, p).start()
            if goes_right(s - 1, p):
                share(b, 8 - s, p)
            if goes_left(s - 1, p) and s < 4 or s == 4 and p == 2:
                share(b, s, p)

    odd_z = z % 2
    PAIRS = (
        (z // 2, 0, (1 + 6 * odd_z) % 8),
        ((z // 2 + 3 + 2 * odd_z) % 4, (7 + 2 * odd_z) % 8, (6 + 4 * odd_z) % 8),
        ((z // 2 + 5 - 2 * odd_z) % 4, (2 + 4 * odd_z) % 8, (3 + 2 * odd_z) % 8),
        ((z // 2 + 2) % 4, 4, (5 + 6 * odd_z) % 8),
    )

    def pair_land(b, j):
        for s in PAIRS[j][1:]:
            for h in range(2):
                sib_copy(b, s, h).wait_recv()
            sib2_copy(b, s).wait_recv()

    def unit(b, j):
        pair_land(b, j)
        ys = PAIRS[j][0]
        gain2 = g2[pl.ds(pl.multiple_of((4 * xh + ys) * KD, KD), KD)].reshape(1, KD)
        cols = pl.ds(pl.multiple_of(ys * KD, KD), KD)
        for r in range(3):
            rows = slice(r * 128, (r + 1) * 128)
            part = mall[b, rows, cols].astype(F32)
            squares_ = jnp.broadcast_to(jnp.sum(part * part, axis=1, keepdims=True), (128, 128))
            ssb[b, rows, :] = squares_ if j == 0 else ssb[b, rows, :] + squares_
            xs[b, rows, cols] = (part * gain2).astype(BF16)
        for m in (1, 2):
            lanes = slice(m * C, (m + 1) * C)
            term = dot(xs[b, :, cols], w2all[m, ys])
            pp[b, :, lanes] = term if j == 0 else pp[b, :, lanes] + term

    def project_queries():
        terms = [dot(xs[b], w2all[0].reshape(4 * KD, C)) for b in range(2)]
        for b in range(2):
            pp[b, :, :C] = terms[b]

    def g_copy(b, m):
        if m == 3:
            return remote(sqs.at[b], sqr.at[b], g_s.at[b, m], g_r.at[b, m], x_far)
        return remote(gs.at[b, m], gr.at[b, m], g_s.at[b, m], g_r.at[b, m], x_far)

    def head_cols(m, h):
        return pl.ds(pl.multiple_of(m * C + h * HEAD, HEAD), HEAD)

    def send_half(b, ms):
        for m in ms:
            gs[b, m] = pp[b, :, head_cols(m, 1 - xh)].astype(BF16)
            g_copy(b, m).start()

    def send_squares(b):
        sqs[b] = jnp.transpose(ssb[b, :T, :])[0:1, :]
        g_copy(b, 3).start()

    def row_factor(b):
        g_copy(b, 3).wait_recv()
        other = jnp.transpose(jnp.broadcast_to(sqr[b], (128, T)))
        ssb[b, :T, :] = lax.rsqrt((ssb[b, :T, :] + other) / D + EPS)

    def head_norm(values):
        values = values.astype(F32)
        return (values * lax.rsqrt(jnp.mean(values * values, axis=1, keepdims=True) + EPS)).astype(BF16)

    def kv_copy(b, d):
        block = kvall.at[y, b]
        side = {1: 0, -1: 1}[d]
        return remote(block, block, kv_s.at[b, side], kv_r.at[b, side], y_peer(d))

    def kv_forward(b, d):
        side = {1: 0, -1: 1}[d]
        part = kvall.at[(y + 4 - d) % 4, b, side]
        return remote(part, part, kv_s.at[b, 2 + side], kv_r.at[b, 2 + side], y_peer(d))

    def kv_pass(b):
        for d in (1, -1):
            kv_copy(b, d).wait_recv()
            kv_forward(b, d).start()

    def kv_land(b):
        for d in (1, -1):
            kv_forward(b, d).wait_recv()

    def joined(b, m):
        g_copy(b, m).wait_recv()
        return ((pp[b, :, head_cols(m, xh)] + gr[b, m].astype(F32)) * ssb[b, :T, :]).astype(BF16)

    def finish_kv(b):
        row_factor(b)
        kvall[y, b, 0] = head_norm(joined(b, 1))
        kvall[y, b, 1] = joined(b, 2)
        for d in (1, -1):
            kv_copy(b, d).start()

    def finish_q(b):
        qbuf[b] = head_norm(joined(b, 0))

    ring_start(0, 0)
    ring_start(0, 1)
    ring_step(0, 1)
    ring_start(1, 0)
    ring_start(1, 1)
    ring_step(0, 2)
    w_pass(1)
    w_send(2)
    ring_step(0, 3)
    ring_step(1, 1)
    ring_step(0, 4)
    ring_step(1, 2)
    w_local.wait()
    w_land(0)
    w_land(1)
    unit(0, 0)
    swap_land(0, 4)
    unit(0, 1)
    unit(0, 2)
    ring_step(1, 3)
    unit(0, 3)
    send_squares(0)
    send_half(0, (1, 2))
    unit(1, 0)
    w_pass(2)
    ring_step(1, 4)
    unit(1, 1)
    swap_land(1, 4)
    unit(1, 2)
    unit(1, 3)
    send_squares(1)
    send_half(1, (1, 2))
    finish_kv(0)
    w_land(2)
    project_queries()
    send_half(0, (0,))
    kv_pass(0)
    finish_kv(1)
    send_half(1, (0,))
    finish_q(0)
    kv_land(0)

    factor = 2.0 * HEAD ** -0.5 * math.log2(math.e)

    def key_block(b, ys, kb, diagonal=False, first=False):
        for qc in range(3):
            rows = slice(qc * 128, (qc + 1) * 128)
            width = (qc + 1) * 128 if diagonal else T
            score = lax.dot_general(
                qbuf[b, rows, :], kvall[ys, kb, 0, :width, :], (((1,), (1,)), ((), ())), preferred_element_type=F32
            )
            weight = jnp.exp2(score * factor)
            if diagonal:
                at = qc * 128 + lax.broadcasted_iota(jnp.int32, (128, width), 0)
                key = lax.broadcasted_iota(jnp.int32, (128, width), 1)
                weight = jnp.where(key <= at, weight, 0.0)
            part = weight[:, :128]
            for n in range(1, width // 128):
                part = part + weight[:, n * 128 : (n + 1) * 128]
            term = dot(weight.astype(BF16), kvall[ys, kb, 1, :width, :])
            if first:
                den[b, rows, :] = part
                num[b, rows, :] = term
            else:
                den[b, rows, :] += part
                num[b, rows, :] += term

    def earlier(b):
        @pl.loop(0, y)
        def _(ys):
            key_block(b, ys, b)

    def o_copy(b, chunk):
        rows = slice(chunk * 128, (chunk + 1) * 128)
        return remote(oloc.at[b, rows, :], obuf.at[rows, :], o_s.at[chunk], o_r.at[chunk], x_far)

    here = pl.ds(pl.multiple_of(xh * HEAD, HEAD), HEAD)
    there = pl.ds(pl.multiple_of((1 - xh) * HEAD, HEAD), HEAD)

    def conclude(b):
        for chunk in range(3):
            rows = slice(chunk * 128, (chunk + 1) * 128)
            out = num[b, rows, :] / jnp.sum(den[b, rows, :], axis=1, keepdims=True)
            oloc[b, rows, :] = out.astype(BF16)

            @pl.when(xh == 1 - b)
            def _():
                o_copy(b, chunk).start()

            @pl.when(xh == b)
            def _():
                att_out[rows, here] = oloc[b, rows, :]

    key_block(0, y, 0, diagonal=True, first=True)
    earlier(0)
    conclude(0)
    kv_pass(1)
    finish_q(1)
    key_block(1, 0, 0, first=True)

    @pl.loop(1, 4)
    def _(ys):
        key_block(1, ys, 0)

    key_block(1, y, 1, diagonal=True)
    kv_land(1)
    earlier(1)
    conclude(1)
    for chunk in range(3):
        o_copy(0, chunk).wait_recv()
    att_out[:, there] = obuf[...]

    @pl.when(c < 7)
    def _():
        id_copy().wait_send()

    for e in range(2):
        same, _, _, cp = sc_copy(e)

        @pl.when(jnp.logical_not(same))
        def _():
            cp.wait_send()

    for a in range(2):
        me = (xl == xh) & (xl == a)

        @pl.when(jnp.logical_not(me))
        def _():
            for h in range(2):
                e1_copy(a, h)[2].wait_send()

    for part in range(3):
        for d in (1, -1):
            w_copy(part, d).wait_send()
            w_forward(part, d).wait_send()
    for d in order:
        az_copy(d).wait_send()
    for d in (0,) + order:
        ax_copy(d).wait_send()
        ac_copy(d, 0).wait_send()
        ac_copy(d, 1).wait_send()
    for d in range(1, 8):
        for kind in range(2):
            ag_copy(kind, d).wait_send()
    for hv in range(2):
        rs_each(hv, range(3), lambda copy: copy.wait_send())
    for b in range(2):
        for s in range(4):
            for p in range(3):
                if goes_right(s, p):
                    zr_copy(b, s, p).wait_send()
                if goes_left(s, p):
                    zl_copy(b, s, p).wait_send()
        for s in range(8):
            for h in range(2):
                sib_copy(b, s, h).wait_send()
            sib2_copy(b, s).wait_send()
            swap_copy(b, s).wait_send()
        for m in range(4):
            g_copy(b, m).wait_send()
        for d in (1, -1):
            kv_copy(b, d).wait_send()
            kv_forward(b, d).wait_send()
    for chunk in range(3):
        o_copy(0, chunk).wait_send()


def hand_over(mixed, att, mixed_out, att_out):
    mixed_out[...] = mixed[...]
    att_out[...] = att[...]


def local(base_ids, embedding, first_gain, hyena_weight, short_filter, long_filter, second_gain, attn_weight):
    dma = pltpu.SemaphoreType.DMA
    vmem = pltpu.VMEM
    scratch = [
        vmem((T,), jnp.int32),
        vmem((2, V, 2 * C), BF16),
        vmem((256, KD), BF16),
        vmem((V, 2 * C), BF16),
        vmem((V, C), BF16),
        vmem((2, 1, 256), F32),
        vmem((8, 64, 2 * C), BF16),
        vmem((8, 64, C), BF16),
        vmem((8, 1, 256), F32),
        vmem((V, 2 * C), BF16),
        vmem((V, C), BF16),
        vmem((640, 3 * C), F32),
        vmem((2, 512, 128), F32),
        vmem((LONG, 128), F32),
        vmem((2, 3, LONG // 2, 128), F32),
        vmem((88, 8, 128), F32),
        vmem((88, 8, 128), F32),
        vmem((88, 8, 128), F32),
        vmem((25, 8, 128), F32),
        vmem((T, 128), F32),
        vmem((2, T, 128), BF16),
        vmem((3, 4, KD, C), BF16),
        vmem((2, T, 16 * C), BF16),
        vmem((2, T, 16 * C), BF16),
        vmem((2, T, 3 * C), F32),
        vmem((2, V, 128), F32),
        vmem((2, 3, T, HEAD), BF16),
        vmem((2, 3, T, HEAD), BF16),
        vmem((2, 1, T), F32),
        vmem((2, 1, T), F32),
        vmem((2, T, HEAD), BF16),
        vmem((4, 2, 2, T, HEAD), BF16),
        vmem((2, T, HEAD), F32),
        vmem((2, T, HEAD), F32),
        vmem((2, T, HEAD), BF16),
        vmem((T, HEAD), BF16),
        dma, dma,
        dma((2,)), dma((2,)),
        dma((8,)), dma((8,)),
        dma((8,)), dma((8,)),
        dma((2, 8)), dma((2, 8)),
        dma((3, 2, 4)), dma((3, 8)),
        dma((2, 7)), dma((2, 7)),
        dma((3, 2, 2)), dma((3, 2, 2)), dma,
        dma((2, 2)), dma((2, 2)),
        dma((2, 4, 3)), dma((2, 4, 3)),
        dma((2, 4, 3)), dma((2, 4, 3)),
        dma((2, 8)), dma((2, 8)),
        dma((2, 8, 3)), dma((2, 8, 3)),
        dma((2, 4)), dma((2, 4)),
        dma((2, 4)), dma((2, 4)),
        dma((3,)), dma((3,)),
    ]
    results = pl.pallas_call(
        kernel,
        out_shape=(jax.ShapeDtypeStruct((T, C), BF16), jax.ShapeDtypeStruct((T, C), BF16)),
        in_specs=[pl.BlockSpec(memory_space=pltpu.VMEM)] * 8,
        out_specs=(pl.BlockSpec(memory_space=pltpu.VMEM), pl.BlockSpec(memory_space=pltpu.VMEM)),
        scratch_shapes=scratch,
        compiler_params=pltpu.CompilerParams(
            collective_id=0, has_side_effects=True, vmem_limit_bytes=56 << 20
        ),
    )(
        base_ids,
        embedding,
        first_gain,
        jnp.transpose(hyena_weight, (1, 0, 2)),
        short_filter,
        long_filter,
        second_gain,
        jnp.transpose(attn_weight, (1, 0, 2)),
    )
    shape = jax.ShapeDtypeStruct((T, C), BF16)
    return pl.pallas_call(hand_over, out_shape=(shape, shape))(*results)


def solution(mesh):
    return jax.shard_map(
        local,
        mesh=mesh,
        in_specs=(
            P("ctx"),
            P(None, "fsdp"),
            P(),
            P("ctx", None, "fsdp"),
            P(None, None, "fsdp"),
            P(None, "fsdp"),
            P(),
            P("ctx", None, "fsdp"),
        ),
        out_specs=(P("ctx", "fsdp"), P("ctx", "fsdp")),
        check_vma=False,
    )
```

```python
import math

import jax
import jax.numpy as jnp
from jax import lax
from jax.experimental import pallas as pl
from jax.experimental.pallas import tpu as pltpu
from jax.sharding import PartitionSpec as P

MESH = pl.DeviceIdType.MESH
F32, BF16 = jnp.float32, jnp.bfloat16
T = 384
V = 512
C = 256
KD = 1024
D = 8192
HEAD = 128
LONG = 128
EPS = 1e-6


def dot(a, b):
    return jnp.dot(a, b, preferred_element_type=F32)


def kernel(
    ids, emb, g1, w1, sf, lf, g2, w2,
    mixed_out, att_out,
    idbuf, ebuf, xbuf, pkv, pq, psq, rskv, rsq, rssq, tkv, tq, sbuf, prbuf, taps, coef, xo, xu, xsum, dv, lcbuf, mbuf,
    w2all, mall, xs, pp, ssb, gs, gr, sqs, sqr, qbuf, kt, vv, num, den, oloc, obuf,
    id_s, id_r, sc_s, sc_r, az_s, az_r, ax_s, ax_r, ac_s, ac_r,
    rs_s, rs_r, ag_s, ag_r, w_s, w_r, wl_s, e1_s, e1_r, zr_s, zr_r, zl_s, zl_r, sw_s, sw_r, sib_s, sib_r,
    g_s, g_r, kv_s, kv_r, o_s, o_r,
):
    c = lax.axis_index("ctx")
    f = lax.axis_index("fsdp")
    xh, y = c // 4, c % 4
    xl, z, k = f // 16, (f // 2) % 8, f % 2

    def dev(xh_, y_, xl_, z_, k_):
        return (xh_ * 4 + y_, xl_ * 16 + z_ * 2 + k_)

    def ctx_peer(d):
        return ((c + d) % 8, f)

    def z_peer(d):
        return dev(xh, y, xl, (z + d) % 8, k)

    def y_peer(d):
        return dev(xh, (y + d) % 4, xl, z, k)

    x_sib = dev(xh, y, 1 - xl, z, k)
    core_sib = dev(xh, y, xl, z, 1 - k)
    x_far = dev(1 - xh, y, xl, z, k)

    def remote(src, dst, ss, rs, to):
        return pltpu.make_async_remote_copy(
            src_ref=src, dst_ref=dst, send_sem=ss, recv_sem=rs, device_id=to, device_id_type=MESH
        )

    barrier = pltpu.get_barrier_semaphore()
    count = 0
    peers = [ctx_peer(d) for d in range(1, 8)] + [z_peer(d) for d in (1, 7, 2, 6)] + [x_sib, core_sib]
    peers += [dev(xl, z // 2, xh, 2 * ((2 * (z // 2) + 6 - y) % 4) + e, k) for e in range(2)]
    peers += [dev(xl, (2 * y + 6 - z // 2) % 4, xh, 2 * y + e, k) for e in range(2)]
    peers += [dev(xl, y, a, z, k) for a in range(2)]
    peers += [dev(a, y, xh, z, k) for a in range(2)]
    for p in peers:
        pl.semaphore_signal(barrier, inc=1, device_id=p, device_id_type=MESH)
        count += 1
    pl.semaphore_wait(barrier, count)

    def id_copy():
        return remote(ids, idbuf, id_s, id_r, ctx_peer(1))

    @pl.when(c < 7)
    def _():
        id_copy().start()

    rows_of = lambda xl_, z_: pl.ds(pl.multiple_of(xl_ * 256 + (z_ % 4) * 64, 64), 64)

    def sc_copy(e):
        to_z = 2 * ((2 * (z // 2) + 6 - y) % 4) + e
        rows = rows_of(xh, to_z)
        cols = pl.ds(pl.multiple_of((z % 2) * C, C), C)
        src, dst = emb.at[rows, :], ebuf.at[k, rows, cols]
        same = (xl == xh) & (z // 2 == y) & (to_z == z)
        return same, src, dst, remote(src, dst, sc_s.at[e], sc_r.at[z % 2], dev(xl, z // 2, xh, to_z, k))

    for e in range(2):
        same, src, dst, cp = sc_copy(e)

        @pl.when(same)
        def _():
            pltpu.make_async_copy(src, dst, sc_r.at[z % 2]).start()

        @pl.when(jnp.logical_not(same))
        def _():
            cp.start()

    W_PARTS = ((1, 3, 0, 512), (1, 3, 512, 512), (0, 1, 0, 512), (0, 1, 512, 512))

    def w_copy(part, d):
        m0, m1, row, count_ = W_PARTS[part]
        side = {1: 0, -1: 1}[d]
        cut = (slice(m0, m1), slice(row, row + count_), slice(None))
        return remote(
            w2.at[cut], w2all.at[cut[0], y, cut[1]], w_s.at[part, 0, side], w_r.at[part, 0, side], y_peer(d)
        )

    def w_forward(part, d):
        m0, m1, row, count_ = W_PARTS[part]
        side = {1: 0, -1: 1}[d]
        half = count_ // 2
        piece = w2all.at[m0:m1, (y - d) % 4, row + side * half : row + (side + 1) * half, :]
        return remote(piece, piece, w_s.at[part, 1, side], w_r.at[part, 1, side], y_peer(d))

    def w_send(part):
        for d in (1, -1):
            w_copy(part, d).start()

    def w_pass(part):
        for d in (1, -1):
            w_copy(part, d).wait_recv()
            w_forward(part, d).start()

    def w_land(part):
        for d in (1, -1):
            w_forward(part, d).wait_recv()

    w_local = pltpu.make_async_copy(w2, w2all.at[:, y], wl_s)
    w_local.start()
    w_send(0)

    def taps_of(lt):
        taps[...] = lf[:, lt * 128 : (lt + 1) * 128]
        even, odd = taps[pl.ds(0, LONG // 2, stride=2), :], taps[pl.ds(1, LONG // 2, stride=2), :]
        coef[lt, 0] = even
        coef[lt, 1] = odd
        coef[lt, 2] = even + odd

    taps_of(0)
    taps_of(1)

    for zb in range(2):
        rows = rows_of(xl, z)
        piece = ebuf.at[k, rows, pl.ds(zb * C, C)]
        remote(piece, piece, sc_s.at[zb], sc_r.at[zb], core_sib).wait_recv()

    def az_copy(d):
        piece = ebuf.at[k, rows_of(xl, z), :]
        return remote(piece, piece, az_s.at[d], az_r.at[d], z_peer(d))

    def ax_copy(d):
        piece = ebuf.at[k, rows_of(xl, (z - d) % 8), :]
        return remote(piece, piece, ax_s.at[d], ax_r.at[d], x_sib)

    def ac_copy(d, s):
        xl_ = (xl + s) % 2
        piece = ebuf.at[k, rows_of(xl_, (z - d) % 8), :]
        return remote(piece, piece, ac_s.at[s, d], ac_r.at[s, d], core_sib)

    order = (1, 7, 2)
    for d in order:
        az_copy(d).start()
    ax_copy(0).start()
    ac_copy(0, 0).start()
    for d in order:
        az_copy(d).wait_recv()
        ax_copy(d).start()
        ac_copy(d, 0).start()
    gain = g1[pl.ds(pl.multiple_of(c * KD, KD), KD)].reshape(1, KD)
    mine = pl.ds(pl.multiple_of(c * 64, 64), 64)

    def half_rows(hv):
        return pl.ds(pl.multiple_of(((xl + hv) % 2) * 256, 256), 256)

    def table(hv):
        rows = half_rows(hv)
        squares = jnp.zeros((256, 1), F32)
        for q in range(4):
            e = ebuf[q % 2, rows, (q // 2) * C : (q // 2 + 1) * C].astype(F32)
            squares = squares + jnp.sum(e * e, axis=1, keepdims=True)
            xbuf[:, q * C : (q + 1) * C] = (e * gain[:, q * C : (q + 1) * C]).astype(BF16)
        psq[hv] = jnp.transpose(jnp.broadcast_to(squares, (256, 128)))[0:1, :]
        terms = [dot(xbuf[...], w1[m]).astype(BF16) for m in (1, 2, 0)]
        pkv[rows, :C] = terms[0]
        pkv[rows, C:] = terms[1]
        pq[rows, :] = terms[2]

    def rs_copy(kind, hv, dy):
        half = (xl + hv) % 2
        to = half * 4 + (y + dy) % 4
        rows = pl.ds(pl.multiple_of(to * 64, 64), 64)
        src = (pkv.at[rows, :], pq.at[rows, :], psq.at[hv])[kind]
        dst = (rskv, rsq, rssq)[kind].at[c]
        return remote(src, dst, rs_s.at[kind, hv, dy], rs_r.at[kind, c], (to, f))

    def rs_each(hv, kinds, act):
        for kind in kinds:
            for dy in (2, 1, 3):
                act(rs_copy(kind, hv, dy))

            @pl.when((xl + hv) % 2 != xh)
            def _():
                act(rs_copy(kind, hv, 0))

    def rs_land(kind):
        slots = []
        for dx in (0, 1):
            for dy in (0, 1, 2, 3):
                if (dx, dy) != (0, 0):
                    slot = ((xh + dx) % 2) * 4 + (y + dy) % 4
                    src = (pkv.at[mine, :], pq.at[mine, :], psq.at[0])[kind]
                    dst = (rskv, rsq, rssq)[kind].at[slot]
                    remote(src, dst, rs_s.at[kind, 0, 0], rs_r.at[kind, slot], core_sib).wait_recv()
                    slots.append(slot)
        return slots

    def ag_copy(kind, d):
        piece = (tkv, tq)[kind].at[mine, :]
        return remote(piece, piece, ag_s.at[kind, d - 1], ag_r.at[kind, d - 1], ctx_peer(d))

    ctx_order = (4, 1, 7, 2, 6, 3, 5)
    for d in (0,) + order:
        ac_copy(d, 0).wait_recv()
    table(0)
    rs_each(0, (2, 0, 1), lambda copy: copy.start())
    for d in (0,) + order:
        ax_copy(d).wait_recv()
        ac_copy(d, 1).start()
    for d in (0,) + order:
        ac_copy(d, 1).wait_recv()
    table(1)
    rs_each(1, (2, 0, 1), lambda copy: copy.start())
    sq = psq[(xl + xh) % 2]
    for slot in rs_land(2):
        sq = sq + rssq[slot]
    row = lax.rsqrt(sq / D + EPS)
    ssb[0, :256, :] = jnp.transpose(jnp.broadcast_to(row, (128, 256)))
    scale_row = ssb[0, pl.ds(pl.multiple_of(y * 64, 64), 64), :][:, 0:1]
    total = pkv[mine, :].astype(F32)
    for slot in rs_land(0):
        total = total + rskv[slot].astype(F32)
    tkv[mine, :] = (total * scale_row).astype(BF16)
    for d in ctx_order:
        ag_copy(0, d).start()
    total = pq[mine, :].astype(F32)
    for slot in rs_land(1):
        total = total + rsq[slot].astype(F32)
    tq[mine, :] = (total * scale_row).astype(BF16)
    for d in ctx_order:
        ag_copy(1, d).start()

    @pl.when(c > 0)
    def _():
        id_copy().wait_recv()

    @pl.when(c == 0)
    def _():
        idbuf[...] = jnp.full(idbuf.shape, -1, jnp.int32)

    for d in ctx_order:
        ag_copy(0, d).wait_recv()

    w_pass(0)
    w_send(1)
    def one_hot(chunk):
        row = idbuf[128 + chunk * 128 : 256 + chunk * 128] if chunk < 2 else ids[(chunk - 2) * 128 : (chunk - 1) * 128]
        words = lax.broadcasted_iota(jnp.int32, (V, 128), 0)
        return jnp.where(words == row.reshape(1, 128), 1.0, 0.0).astype(BF16)

    def pick(hot, values):
        return lax.dot_general(hot, values, (((0,), (0,)), ((), ())), preferred_element_type=F32)

    for chunk in range(5):
        sbuf[chunk * 128 : (chunk + 1) * 128, C:] = pick(one_hot(chunk), tkv[...])

    def short(m, start, size, lanes=slice(0, C)):
        cols = slice(m * C + lanes.start, m * C + lanes.stop)
        out = sf[0, m : m + 1, lanes] * sbuf[start : start + size, cols]
        for j in range(1, 3):
            out = out + sf[j, m : m + 1, lanes] * sbuf[start - j : start - j + size, cols]
        return out

    for chunk in range(4):
        prod = (short(1, 128 + chunk * 128, 128) * short(2, 128 + chunk * 128, 128)).astype(BF16).astype(F32)
        for lt in range(2):
            prbuf[lt, chunk * 128 : (chunk + 1) * 128, :] = prod[:, lt * 128 : (lt + 1) * 128]

    def cols_of(z_, k_, h):
        return pl.ds(pl.multiple_of((z_ * 2 + k_) * C + h * 128, 128), 128)

    def rows_at(h, half):
        return pl.ds(0, T) if h == 1 else pl.ds(pl.multiple_of(half * (T // 2), T // 2), T // 2)

    def e1_copy(a, h):
        dst = mall.at[xh, rows_at(h, a), cols_of(z, k, h)]
        src = mbuf.at[h, rows_at(h, a), :]
        return src, dst, remote(src, dst, e1_s.at[a, h], e1_r.at[xh, h], dev(xl, y, a, z, k))

    def e1_send(h):
        for a in range(2):
            src, dst, cp = e1_copy(a, h)
            me = (xl == xh) & (xl == a)

            @pl.when(me)
            def _():
                pltpu.make_async_copy(src, dst, e1_r.at[xh, h]).start()

            @pl.when(jnp.logical_not(me))
            def _():
                cp.start()

    LANE_T = T // 8

    def half_filter(lt, which, src, start, count_):
        def eight(k8, acc):
            window = src[pl.ds(start + 56 - 8 * k8, count_ + 7)]
            row = coef[lt, which, pl.ds(pl.multiple_of(8 * k8, 8), 8), :]
            for jj in range(8):
                acc = acc + row[jj : jj + 1, :][None] * window[7 - jj : count_ + 7 - jj]
            return acc

        return lax.fori_loop(0, LONG // 16, eight, jnp.zeros((count_, 8, 128), F32), unroll=True)

    def convolve(lt):
        xu[0] = prbuf[lt, pl.ds(1, 8, stride=LANE_T), :]
        for m in range(87):
            odd = prbuf[lt, pl.ds(2 * m + 2, 8, stride=LANE_T), :]
            even = prbuf[lt, pl.ds(2 * m + 3, 8, stride=LANE_T), :]
            xo[m] = odd
            xu[m + 1] = even
            xsum[m] = odd + even
        dv[0:13] = half_filter(lt, 1, xu, 0, 13)
        dv[13:25] = half_filter(lt, 1, xu, 13, 12)
        for g in range(2):
            a = half_filter(lt, 0, xo, 12 * g, 12)
            t = half_filter(lt, 2, xsum, 12 * g, 12)
            for i in range(12):
                n = 12 * g + i
                lcbuf[pl.ds(2 * n, 8, stride=LANE_T), :] = a[i] + dv[n]
                lcbuf[pl.ds(2 * n + 1, 8, stride=LANE_T), :] = t[i] - a[i] - dv[n + 1]

    def residual(lt):
        lanes = slice(lt * 128, (lt + 1) * 128)
        for chunk in range(3):
            rows = slice(chunk * 128, (chunk + 1) * 128)
            features = pick(one_hot(chunk + 2), emb[:, lanes])
            gate = short(0, 256 + chunk * 128, 128, lanes)
            mixed = (features + gate * lcbuf[rows, :]).astype(BF16)
            mbuf[lt, rows, :] = mixed
            mixed_out[rows, lanes] = mixed

    convolve(0)
    for d in ctx_order:
        ag_copy(1, d).wait_recv()
    for chunk in range(1, 5):
        sbuf[chunk * 128 : (chunk + 1) * 128, :C] = pick(one_hot(chunk), tq[...])
    residual(0)
    e1_send(0)
    convolve(1)
    residual(1)
    e1_send(1)

    def chunk_of(b, z_, p):
        rows = rows_at(0, xl) if p == 2 else pl.ds(p * (T // 2), T // 2)
        return mall.at[b, rows, cols_of(z_, k, 1 - p // 2)]

    def zr_copy(b, s, p):
        piece = chunk_of(b, (z + 8 - s) % 8, p)
        return remote(piece, piece, zr_s.at[b, s, p], zr_r.at[b, s, p], z_peer(1))

    def zl_copy(b, s, p):
        piece = chunk_of(b, (z + s) % 8, p)
        return remote(piece, piece, zl_s.at[b, s, p], zl_r.at[b, s, p], z_peer(-1))

    def sib_copy(b, s, h):
        piece = mall.at[b, rows_at(h, xl), cols_of((z + s) % 8, k, h)]
        return remote(piece, piece, sib_s.at[b, s, h], sib_r.at[b, s, h], core_sib)

    def swap_copy(b, s):
        piece = mall.at[b, rows_at(0, xl), cols_of((z + s) % 8, k, 0)]
        return remote(piece, piece, sw_s.at[b, s], sw_r.at[b, s], x_sib)

    def sib2_copy(b, s):
        piece = mall.at[b, rows_at(0, 1 - xl), cols_of((z + s) % 8, k, 0)]
        return remote(piece, piece, sib_s.at[b, s, 2], sib_r.at[b, s, 2], core_sib)

    def share(b, s, p):
        if p > 0:
            sib_copy(b, s, 2 - p).start()
        if p == 2:
            swap_copy(b, s).start()

    def swap_land(b, s):
        swap_copy(b, s).wait_recv()
        sib2_copy(b, s).start()

    def ring_start(b, h):
        piece = mall.at[b, rows_at(h, xl), cols_of(z, k, h)]
        remote(piece, piece, e1_s.at[0, h], e1_r.at[b, h], core_sib).wait_recv()
        for p in ((2,), (0, 1))[h]:
            zr_copy(b, 0, p).start()
            zl_copy(b, 0, p).start()
        share(b, 0, 2 - h)

    def goes_right(s, p):
        return s < 3 or (s == 3 and p < 2)

    def goes_left(s, p):
        return s < 3 or (s == 3 and p == 2)

    def ring_step(b, s):
        for near in ((0,), (7, 1), (6, 2), (5, 3))[s - 1]:
            swap_land(b, near)
        for p in (2, 0, 1):
            if goes_right(s - 1, p):
                zr_copy(b, s - 1, p).wait_recv()
                if goes_right(s, p):
                    zr_copy(b, s, p).start()
            if goes_left(s - 1, p):
                zl_copy(b, s - 1, p).wait_recv()
                if goes_left(s, p):
                    zl_copy(b, s, p).start()
            if goes_right(s - 1, p):
                share(b, 8 - s, p)
            if goes_left(s - 1, p) and s < 4 or s == 4 and p == 2:
                share(b, s, p)

    odd_z = z % 2
    PAIRS = (
        (z // 2, 0, (1 + 6 * odd_z) % 8),
        ((z // 2 + 3 + 2 * odd_z) % 4, (7 + 2 * odd_z) % 8, (6 + 4 * odd_z) % 8),
        ((z // 2 + 5 - 2 * odd_z) % 4, (2 + 4 * odd_z) % 8, (3 + 2 * odd_z) % 8),
        ((z // 2 + 2) % 4, 4, (5 + 6 * odd_z) % 8),
    )

    def pair_land(b, j):
        for s in PAIRS[j][1:]:
            for h in range(2):
                sib_copy(b, s, h).wait_recv()
            sib2_copy(b, s).wait_recv()

    def unit(b, j):
        pair_land(b, j)
        ys = PAIRS[j][0]
        gain2 = g2[pl.ds(pl.multiple_of((4 * xh + ys) * KD, KD), KD)].reshape(1, KD)
        cols = pl.ds(pl.multiple_of(ys * KD, KD), KD)
        for r in range(3):
            rows = slice(r * 128, (r + 1) * 128)
            part = mall[b, rows, cols].astype(F32)
            squares_ = jnp.broadcast_to(jnp.sum(part * part, axis=1, keepdims=True), (128, 128))
            ssb[b, rows, :] = squares_ if j == 0 else ssb[b, rows, :] + squares_
            xs[b, rows, cols] = (part * gain2).astype(BF16)
        for m in (1, 2):
            lanes = slice(m * C, (m + 1) * C)
            term = dot(xs[b, :, cols], w2all[m, ys])
            pp[b, :, lanes] = term if j == 0 else pp[b, :, lanes] + term

    def project_queries():
        terms = [dot(xs[b], w2all[0].reshape(4 * KD, C)) for b in range(2)]
        for b in range(2):
            pp[b, :, :C] = terms[b]

    def g_copy(b, m):
        if m == 3:
            return remote(sqs.at[b], sqr.at[b], g_s.at[b, m], g_r.at[b, m], x_far)
        return remote(gs.at[b, m], gr.at[b, m], g_s.at[b, m], g_r.at[b, m], x_far)

    def head_cols(m, h):
        return pl.ds(pl.multiple_of(m * C + h * HEAD, HEAD), HEAD)

    def send_half(b, ms):
        for m in ms:
            gs[b, m] = pp[b, :, head_cols(m, 1 - xh)].astype(BF16)
            g_copy(b, m).start()

    def send_squares(b):
        sqs[b] = jnp.transpose(ssb[b, :T, :])[0:1, :]
        g_copy(b, 3).start()

    def row_factor(b):
        g_copy(b, 3).wait_recv()
        other = jnp.transpose(jnp.broadcast_to(sqr[b], (128, T)))
        ssb[b, :T, :] = lax.rsqrt((ssb[b, :T, :] + other) / D + EPS)

    def head_norm(values):
        values = values.astype(F32)
        return (values * lax.rsqrt(jnp.mean(values * values, axis=1, keepdims=True) + EPS)).astype(BF16)

    def kv_copy(b, d, part):
        block = (kt, vv)[part].at[y, b]
        side = {1: 0, -1: 1}[d]
        return remote(block, block, kv_s.at[b, part, side], kv_r.at[b, part, side], y_peer(d))

    def kv_forward(b, d):
        side = {1: 0, -1: 1}[d]
        part = (kt, vv)[side].at[(y + 4 - d) % 4, b]
        return remote(part, part, kv_s.at[b, 2, side], kv_r.at[b, 2, side], y_peer(d))

    def kv_pass(b):
        for d in (1, -1):
            kv_copy(b, d, 0 if d == 1 else 1).wait_recv()
            kv_forward(b, d).start()
        for d in (1, -1):
            kv_copy(b, d, 1 if d == 1 else 0).wait_recv()

    def kv_land(b):
        for d in (1, -1):
            kv_forward(b, d).wait_recv()

    def joined(b, m):
        g_copy(b, m).wait_recv()
        return ((pp[b, :, head_cols(m, xh)] + gr[b, m].astype(F32)) * ssb[b, :T, :]).astype(BF16)

    def finish_kv(b):
        row_factor(b)
        kt[y, b] = jnp.transpose(head_norm(joined(b, 1)))
        vv[y, b] = joined(b, 2)
        for part in range(2):
            for d in (1, -1):
                kv_copy(b, d, part).start()

    def finish_q(b):
        qbuf[b] = head_norm(joined(b, 0))

    ring_start(0, 0)
    ring_start(0, 1)
    ring_step(0, 1)
    ring_start(1, 0)
    ring_start(1, 1)
    ring_step(0, 2)
    w_pass(1)
    w_send(2)
    ring_step(0, 3)
    ring_step(1, 1)
    w_send(3)
    ring_step(0, 4)
    ring_step(1, 2)
    w_local.wait()
    w_land(0)
    w_land(1)
    unit(0, 0)
    swap_land(0, 4)
    unit(0, 1)
    unit(0, 2)
    ring_step(1, 3)
    w_pass(2)
    unit(0, 3)
    send_squares(0)
    send_half(0, (1, 2))
    unit(1, 0)
    ring_step(1, 4)
    unit(1, 1)
    w_pass(3)
    finish_kv(0)
    swap_land(1, 4)
    unit(1, 2)
    unit(1, 3)
    send_squares(1)
    send_half(1, (1, 2))
    w_land(2)
    w_land(3)
    project_queries()
    send_half(0, (0,))
    kv_pass(0)
    finish_kv(1)
    send_half(1, (0,))
    finish_q(0)
    kv_land(0)

    factor = 2.0 * HEAD ** -0.5 * math.log2(math.e)

    def key_block(b, ys, kb, diagonal=False, first=False):
        for qc in range(3):
            rows = slice(qc * 128, (qc + 1) * 128)
            width = (qc + 1) * 128 if diagonal else T
            score = dot(qbuf[b, rows, :], kt[ys, kb, :, :width])
            weight = jnp.exp2(score * factor)
            if diagonal:
                at = qc * 128 + lax.broadcasted_iota(jnp.int32, (128, width), 0)
                key = lax.broadcasted_iota(jnp.int32, (128, width), 1)
                weight = jnp.where(key <= at, weight, 0.0)
            part = weight[:, :128]
            for n in range(1, width // 128):
                part = part + weight[:, n * 128 : (n + 1) * 128]
            term = dot(weight.astype(BF16), vv[ys, kb, :width, :])
            if first:
                den[b, rows, :] = part
                num[b, rows, :] = term
            else:
                den[b, rows, :] += part
                num[b, rows, :] += term

    def earlier(b):
        @pl.loop(0, y)
        def _(ys):
            key_block(b, ys, b)

    def o_copy(b, chunk):
        rows = slice(chunk * 128, (chunk + 1) * 128)
        return remote(oloc.at[b, rows, :], obuf.at[rows, :], o_s.at[chunk], o_r.at[chunk], x_far)

    here = pl.ds(pl.multiple_of(xh * HEAD, HEAD), HEAD)
    there = pl.ds(pl.multiple_of((1 - xh) * HEAD, HEAD), HEAD)

    def conclude(b):
        for chunk in range(3):
            rows = slice(chunk * 128, (chunk + 1) * 128)
            out = num[b, rows, :] / jnp.sum(den[b, rows, :], axis=1, keepdims=True)
            oloc[b, rows, :] = out.astype(BF16)

            @pl.when(xh == 1 - b)
            def _():
                o_copy(b, chunk).start()

            @pl.when(xh == b)
            def _():
                att_out[rows, here] = oloc[b, rows, :]

    key_block(0, y, 0, diagonal=True, first=True)
    earlier(0)
    conclude(0)
    kv_pass(1)
    finish_q(1)
    key_block(1, 0, 0, first=True)

    @pl.loop(1, 4)
    def _(ys):
        key_block(1, ys, 0)

    key_block(1, y, 1, diagonal=True)
    kv_land(1)
    earlier(1)
    conclude(1)
    for chunk in range(3):
        o_copy(0, chunk).wait_recv()
    att_out[:, there] = obuf[...]

    @pl.when(c < 7)
    def _():
        id_copy().wait_send()

    for e in range(2):
        same, _, _, cp = sc_copy(e)

        @pl.when(jnp.logical_not(same))
        def _():
            cp.wait_send()

    for a in range(2):
        me = (xl == xh) & (xl == a)

        @pl.when(jnp.logical_not(me))
        def _():
            for h in range(2):
                e1_copy(a, h)[2].wait_send()

    for part in range(4):
        for d in (1, -1):
            w_copy(part, d).wait_send()
            w_forward(part, d).wait_send()
    for d in order:
        az_copy(d).wait_send()
    for d in (0,) + order:
        ax_copy(d).wait_send()
        ac_copy(d, 0).wait_send()
        ac_copy(d, 1).wait_send()
    for d in range(1, 8):
        for kind in range(2):
            ag_copy(kind, d).wait_send()
    for hv in range(2):
        rs_each(hv, range(3), lambda copy: copy.wait_send())
    for b in range(2):
        for s in range(4):
            for p in range(3):
                if goes_right(s, p):
                    zr_copy(b, s, p).wait_send()
                if goes_left(s, p):
                    zl_copy(b, s, p).wait_send()
        for s in range(8):
            for h in range(2):
                sib_copy(b, s, h).wait_send()
            sib2_copy(b, s).wait_send()
            swap_copy(b, s).wait_send()
        for m in range(4):
            g_copy(b, m).wait_send()
        for d in (1, -1):
            for part in range(2):
                kv_copy(b, d, part).wait_send()
            kv_forward(b, d).wait_send()
    for chunk in range(3):
        o_copy(0, chunk).wait_send()


def hand_over(mixed, att, mixed_out, att_out):
    mixed_out[...] = mixed[...]
    att_out[...] = att[...]


def local(base_ids, embedding, first_gain, hyena_weight, short_filter, long_filter, second_gain, attn_weight):
    dma = pltpu.SemaphoreType.DMA
    vmem = pltpu.VMEM
    scratch = [
        vmem((T,), jnp.int32),
        vmem((2, V, 2 * C), BF16),
        vmem((256, KD), BF16),
        vmem((V, 2 * C), BF16),
        vmem((V, C), BF16),
        vmem((2, 1, 256), F32),
        vmem((8, 64, 2 * C), BF16),
        vmem((8, 64, C), BF16),
        vmem((8, 1, 256), F32),
        vmem((V, 2 * C), BF16),
        vmem((V, C), BF16),
        vmem((640, 3 * C), F32),
        vmem((2, 512, 128), F32),
        vmem((LONG, 128), F32),
        vmem((2, 3, LONG // 2, 128), F32),
        vmem((88, 8, 128), F32),
        vmem((88, 8, 128), F32),
        vmem((88, 8, 128), F32),
        vmem((25, 8, 128), F32),
        vmem((T, 128), F32),
        vmem((2, T, 128), BF16),
        vmem((3, 4, KD, C), BF16),
        vmem((2, T, 16 * C), BF16),
        vmem((2, T, 16 * C), BF16),
        vmem((2, T, 3 * C), F32),
        vmem((2, V, 128), F32),
        vmem((2, 3, T, HEAD), BF16),
        vmem((2, 3, T, HEAD), BF16),
        vmem((2, 1, T), F32),
        vmem((2, 1, T), F32),
        vmem((2, T, HEAD), BF16),
        vmem((4, 2, HEAD, T), BF16),
        vmem((4, 2, T, HEAD), BF16),
        vmem((2, T, HEAD), F32),
        vmem((2, T, HEAD), F32),
        vmem((2, T, HEAD), BF16),
        vmem((T, HEAD), BF16),
        dma, dma,
        dma((2,)), dma((2,)),
        dma((8,)), dma((8,)),
        dma((8,)), dma((8,)),
        dma((2, 8)), dma((2, 8)),
        dma((3, 2, 4)), dma((3, 8)),
        dma((2, 7)), dma((2, 7)),
        dma((4, 2, 2)), dma((4, 2, 2)), dma,
        dma((2, 2)), dma((2, 2)),
        dma((2, 4, 3)), dma((2, 4, 3)),
        dma((2, 4, 3)), dma((2, 4, 3)),
        dma((2, 8)), dma((2, 8)),
        dma((2, 8, 3)), dma((2, 8, 3)),
        dma((2, 4)), dma((2, 4)),
        dma((2, 3, 2)), dma((2, 3, 2)),
        dma((3,)), dma((3,)),
    ]
    results = pl.pallas_call(
        kernel,
        out_shape=(jax.ShapeDtypeStruct((T, C), BF16), jax.ShapeDtypeStruct((T, C), BF16)),
        in_specs=[pl.BlockSpec(memory_space=pltpu.VMEM)] * 8,
        out_specs=(pl.BlockSpec(memory_space=pltpu.VMEM), pl.BlockSpec(memory_space=pltpu.VMEM)),
        scratch_shapes=scratch,
        compiler_params=pltpu.CompilerParams(
            collective_id=0, has_side_effects=True, vmem_limit_bytes=56 << 20
        ),
    )(
        base_ids,
        embedding,
        first_gain,
        jnp.transpose(hyena_weight, (1, 0, 2)),
        short_filter,
        long_filter,
        second_gain,
        jnp.transpose(attn_weight, (1, 0, 2)),
    )
    shape = jax.ShapeDtypeStruct((T, C), BF16)
    return pl.pallas_call(hand_over, out_shape=(shape, shape))(*results)


def solution(mesh):
    return jax.shard_map(
        local,
        mesh=mesh,
        in_specs=(
            P("ctx"),
            P(None, "fsdp"),
            P(),
            P("ctx", None, "fsdp"),
            P(None, None, "fsdp"),
            P(None, "fsdp"),
            P(),
            P("ctx", None, "fsdp"),
        ),
        out_specs=(P("ctx", "fsdp"), P("ctx", "fsdp")),
        check_vma=False,
    )
```

```python
import math

import jax
import jax.numpy as jnp
from jax import lax
from jax.experimental import pallas as pl
from jax.experimental.pallas import tpu as pltpu
from jax.sharding import PartitionSpec as P

MESH = pl.DeviceIdType.MESH
F32, BF16 = jnp.float32, jnp.bfloat16
T = 384
V = 512
C = 256
KD = 1024
D = 8192
HEAD = 128
LONG = 128
EPS = 1e-6


def dot(a, b):
    return jnp.dot(a, b, preferred_element_type=F32)


def kernel(
    ids, emb, g1, w1, sf, lf, g2, w2,
    mixed_out, att_out,
    idbuf, ebuf, xbuf, pkv, pq, psq, rskv, rsq, rssq, tkv, tq, sbuf, prbuf, taps, coef, xo, xu, xsum, dv, lcbuf, mbuf,
    w2all, mall, xs, pp, ssb, gs, gr, sqs, sqr, qbuf, kt, vv, num, den, oloc, obuf,
    id_s, id_r, sc_s, sc_r, az_s, az_r, ax_s, ax_r, ac_s, ac_r,
    rs_s, rs_r, ag_s, ag_r, w_s, w_r, wl_s, e1_s, e1_r, zr_s, zr_r, zl_s, zl_r, sw_s, sw_r, sib_s, sib_r,
    g_s, g_r, kv_s, kv_r, o_s, o_r,
):
    c = lax.axis_index("ctx")
    f = lax.axis_index("fsdp")
    xh, y = c // 4, c % 4
    xl, z, k = f // 16, (f // 2) % 8, f % 2

    def dev(xh_, y_, xl_, z_, k_):
        return (xh_ * 4 + y_, xl_ * 16 + z_ * 2 + k_)

    def ctx_peer(d):
        return ((c + d) % 8, f)

    def z_peer(d):
        return dev(xh, y, xl, (z + d) % 8, k)

    def y_peer(d):
        return dev(xh, (y + d) % 4, xl, z, k)

    x_sib = dev(xh, y, 1 - xl, z, k)
    core_sib = dev(xh, y, xl, z, 1 - k)
    x_far = dev(1 - xh, y, xl, z, k)

    def remote(src, dst, ss, rs, to):
        return pltpu.make_async_remote_copy(
            src_ref=src, dst_ref=dst, send_sem=ss, recv_sem=rs, device_id=to, device_id_type=MESH
        )

    barrier = pltpu.get_barrier_semaphore()
    count = 0
    peers = [ctx_peer(d) for d in range(1, 8)] + [z_peer(d) for d in (1, 7, 2, 6)] + [x_sib, core_sib]
    peers += [dev(xl, z // 2, xh, 2 * ((2 * (z // 2) + 6 - y) % 4) + e, k) for e in range(2)]
    peers += [dev(xl, (2 * y + 6 - z // 2) % 4, xh, 2 * y + e, k) for e in range(2)]
    peers += [dev(xl, y, a, z, k) for a in range(2)]
    peers += [dev(a, y, xh, z, k) for a in range(2)]
    for p in peers:
        pl.semaphore_signal(barrier, inc=1, device_id=p, device_id_type=MESH)
        count += 1
    pl.semaphore_wait(barrier, count)

    def id_copy():
        return remote(ids, idbuf, id_s, id_r, ctx_peer(1))

    @pl.when(c < 7)
    def _():
        id_copy().start()

    rows_of = lambda xl_, z_: pl.ds(pl.multiple_of(xl_ * 256 + (z_ % 4) * 64, 64), 64)

    def sc_copy(e):
        to_z = 2 * ((2 * (z // 2) + 6 - y) % 4) + e
        rows = rows_of(xh, to_z)
        cols = pl.ds(pl.multiple_of((z % 2) * C, C), C)
        src, dst = emb.at[rows, :], ebuf.at[k, rows, cols]
        same = (xl == xh) & (z // 2 == y) & (to_z == z)
        return same, src, dst, remote(src, dst, sc_s.at[e], sc_r.at[z % 2], dev(xl, z // 2, xh, to_z, k))

    for e in range(2):
        same, src, dst, cp = sc_copy(e)

        @pl.when(same)
        def _():
            pltpu.make_async_copy(src, dst, sc_r.at[z % 2]).start()

        @pl.when(jnp.logical_not(same))
        def _():
            cp.start()

    W_PARTS = ((1, 3, 0, 512), (1, 3, 512, 512), (0, 1, 0, 512), (0, 1, 512, 512))

    def w_copy(part, d):
        m0, m1, row, count_ = W_PARTS[part]
        side = {1: 0, -1: 1}[d]
        cut = (slice(m0, m1), slice(row, row + count_), slice(None))
        return remote(
            w2.at[cut], w2all.at[cut[0], y, cut[1]], w_s.at[part, 0, side], w_r.at[part, 0, side], y_peer(d)
        )

    def w_forward(part, d):
        m0, m1, row, count_ = W_PARTS[part]
        side = {1: 0, -1: 1}[d]
        half = count_ // 2
        piece = w2all.at[m0:m1, (y - d) % 4, row + side * half : row + (side + 1) * half, :]
        return remote(piece, piece, w_s.at[part, 1, side], w_r.at[part, 1, side], y_peer(d))

    def w_send(part):
        for d in (1, -1):
            w_copy(part, d).start()

    def w_pass(part):
        for d in (1, -1):
            w_copy(part, d).wait_recv()
            w_forward(part, d).start()

    def w_land(part):
        for d in (1, -1):
            w_forward(part, d).wait_recv()

    w_local = pltpu.make_async_copy(w2, w2all.at[:, y], wl_s)
    w_local.start()
    w_send(0)

    def taps_of(lt):
        taps[...] = lf[:, lt * 128 : (lt + 1) * 128]
        even, odd = taps[pl.ds(0, LONG // 2, stride=2), :], taps[pl.ds(1, LONG // 2, stride=2), :]
        coef[lt, 0] = even
        coef[lt, 1] = odd
        coef[lt, 2] = even + odd

    taps_of(0)
    taps_of(1)

    for zb in range(2):
        rows = rows_of(xl, z)
        piece = ebuf.at[k, rows, pl.ds(zb * C, C)]
        remote(piece, piece, sc_s.at[zb], sc_r.at[zb], core_sib).wait_recv()

    def az_copy(d):
        piece = ebuf.at[k, rows_of(xl, z), :]
        return remote(piece, piece, az_s.at[d], az_r.at[d], z_peer(d))

    def ax_copy(d):
        piece = ebuf.at[k, rows_of(xl, (z - d) % 8), :]
        return remote(piece, piece, ax_s.at[d], ax_r.at[d], x_sib)

    def ac_copy(d, s):
        xl_ = (xl + s) % 2
        piece = ebuf.at[k, rows_of(xl_, (z - d) % 8), :]
        return remote(piece, piece, ac_s.at[s, d], ac_r.at[s, d], core_sib)

    order = (1, 7, 2)
    for d in order:
        az_copy(d).start()
    ax_copy(0).start()
    ac_copy(0, 0).start()
    for d in order:
        az_copy(d).wait_recv()
        ax_copy(d).start()
        ac_copy(d, 0).start()
    gain = g1[pl.ds(pl.multiple_of(c * KD, KD), KD)].reshape(1, KD)
    mine = pl.ds(pl.multiple_of(c * 64, 64), 64)

    def half_rows(hv):
        return pl.ds(pl.multiple_of(((xl + hv) % 2) * 256, 256), 256)

    def table(hv):
        rows = half_rows(hv)
        squares = jnp.zeros((256, 1), F32)
        for q in range(4):
            e = ebuf[q % 2, rows, (q // 2) * C : (q // 2 + 1) * C].astype(F32)
            squares = squares + jnp.sum(e * e, axis=1, keepdims=True)
            xbuf[:, q * C : (q + 1) * C] = (e * gain[:, q * C : (q + 1) * C]).astype(BF16)
        psq[hv] = jnp.transpose(jnp.broadcast_to(squares, (256, 128)))[0:1, :]
        terms = [dot(xbuf[...], w1[m]).astype(BF16) for m in (1, 2, 0)]
        pkv[rows, :C] = terms[0]
        pkv[rows, C:] = terms[1]
        pq[rows, :] = terms[2]

    def rs_copy(kind, hv, dy):
        half = (xl + hv) % 2
        to = half * 4 + (y + dy) % 4
        rows = pl.ds(pl.multiple_of(to * 64, 64), 64)
        src = (pkv.at[rows, :], pq.at[rows, :], psq.at[hv])[kind]
        dst = (rskv, rsq, rssq)[kind].at[c]
        return remote(src, dst, rs_s.at[kind, hv, dy], rs_r.at[kind, c], (to, f))

    def rs_each(hv, kinds, act):
        for kind in kinds:
            for dy in (2, 1, 3):
                act(rs_copy(kind, hv, dy))

            @pl.when((xl + hv) % 2 != xh)
            def _():
                act(rs_copy(kind, hv, 0))

    def rs_land(kind):
        slots = []
        for dx in (0, 1):
            for dy in (0, 1, 2, 3):
                if (dx, dy) != (0, 0):
                    slot = ((xh + dx) % 2) * 4 + (y + dy) % 4
                    src = (pkv.at[mine, :], pq.at[mine, :], psq.at[0])[kind]
                    dst = (rskv, rsq, rssq)[kind].at[slot]
                    remote(src, dst, rs_s.at[kind, 0, 0], rs_r.at[kind, slot], core_sib).wait_recv()
                    slots.append(slot)
        return slots

    def ag_copy(kind, d):
        piece = (tkv, tq)[kind].at[mine, :]
        return remote(piece, piece, ag_s.at[kind, d - 1], ag_r.at[kind, d - 1], ctx_peer(d))

    ctx_order = (4, 1, 7, 2, 6, 3, 5)
    for d in (0,) + order:
        ac_copy(d, 0).wait_recv()
    table(0)
    rs_each(0, (2, 0, 1), lambda copy: copy.start())
    for d in (0,) + order:
        ax_copy(d).wait_recv()
        ac_copy(d, 1).start()
    for d in (0,) + order:
        ac_copy(d, 1).wait_recv()
    table(1)
    rs_each(1, (2, 0, 1), lambda copy: copy.start())
    sq = psq[(xl + xh) % 2]
    for slot in rs_land(2):
        sq = sq + rssq[slot]
    row = lax.rsqrt(sq / D + EPS)
    ssb[0, :256, :] = jnp.transpose(jnp.broadcast_to(row, (128, 256)))
    scale_row = ssb[0, pl.ds(pl.multiple_of(y * 64, 64), 64), :][:, 0:1]
    total = pkv[mine, :].astype(F32)
    for slot in rs_land(0):
        total = total + rskv[slot].astype(F32)
    tkv[mine, :] = (total * scale_row).astype(BF16)
    for d in ctx_order:
        ag_copy(0, d).start()
    total = pq[mine, :].astype(F32)
    for slot in rs_land(1):
        total = total + rsq[slot].astype(F32)
    tq[mine, :] = (total * scale_row).astype(BF16)
    for d in ctx_order:
        ag_copy(1, d).start()

    @pl.when(c > 0)
    def _():
        id_copy().wait_recv()

    @pl.when(c == 0)
    def _():
        idbuf[...] = jnp.full(idbuf.shape, -1, jnp.int32)

    for d in ctx_order:
        ag_copy(0, d).wait_recv()

    w_pass(0)
    w_send(1)
    def one_hot(chunk):
        row = idbuf[128 + chunk * 128 : 256 + chunk * 128] if chunk < 2 else ids[(chunk - 2) * 128 : (chunk - 1) * 128]
        words = lax.broadcasted_iota(jnp.int32, (V, 128), 0)
        return jnp.where(words == row.reshape(1, 128), 1.0, 0.0).astype(BF16)

    def pick(hot, values):
        return lax.dot_general(hot, values, (((0,), (0,)), ((), ())), preferred_element_type=F32)

    for chunk in range(5):
        sbuf[chunk * 128 : (chunk + 1) * 128, C:] = pick(one_hot(chunk), tkv[...])

    def short(m, start, size, lanes=slice(0, C)):
        cols = slice(m * C + lanes.start, m * C + lanes.stop)
        out = sf[0, m : m + 1, lanes] * sbuf[start : start + size, cols]
        for j in range(1, 3):
            out = out + sf[j, m : m + 1, lanes] * sbuf[start - j : start - j + size, cols]
        return out

    for chunk in range(4):
        prod = (short(1, 128 + chunk * 128, 128) * short(2, 128 + chunk * 128, 128)).astype(BF16).astype(F32)
        for lt in range(2):
            prbuf[lt, chunk * 128 : (chunk + 1) * 128, :] = prod[:, lt * 128 : (lt + 1) * 128]

    def cols_of(z_, k_, h):
        return pl.ds(pl.multiple_of((z_ * 2 + k_) * C + h * 128, 128), 128)

    def rows_at(h, half):
        return pl.ds(0, T) if h == 1 else pl.ds(pl.multiple_of(half * (T // 2), T // 2), T // 2)

    def e1_copy(a, h):
        dst = mall.at[xh, rows_at(h, a), cols_of(z, k, h)]
        src = mbuf.at[h, rows_at(h, a), :]
        return src, dst, remote(src, dst, e1_s.at[a, h], e1_r.at[xh, h], dev(xl, y, a, z, k))

    def e1_send(h):
        for a in range(2):
            src, dst, cp = e1_copy(a, h)
            me = (xl == xh) & (xl == a)

            @pl.when(me)
            def _():
                pltpu.make_async_copy(src, dst, e1_r.at[xh, h]).start()

            @pl.when(jnp.logical_not(me))
            def _():
                cp.start()

    LANE_T = T // 8

    def half_filter(lt, which, src, start, count_):
        def eight(k8, acc):
            window = src[pl.ds(start + 56 - 8 * k8, count_ + 7)]
            row = coef[lt, which, pl.ds(pl.multiple_of(8 * k8, 8), 8), :]
            for jj in range(8):
                acc = acc + row[jj : jj + 1, :][None] * window[7 - jj : count_ + 7 - jj]
            return acc

        return lax.fori_loop(0, LONG // 16, eight, jnp.zeros((count_, 8, 128), F32), unroll=True)

    def convolve(lt):
        xu[0] = prbuf[lt, pl.ds(1, 8, stride=LANE_T), :]
        for m in range(87):
            odd = prbuf[lt, pl.ds(2 * m + 2, 8, stride=LANE_T), :]
            even = prbuf[lt, pl.ds(2 * m + 3, 8, stride=LANE_T), :]
            xo[m] = odd
            xu[m + 1] = even
            xsum[m] = odd + even
        dv[0:13] = half_filter(lt, 1, xu, 0, 13)
        dv[13:25] = half_filter(lt, 1, xu, 13, 12)
        for g in range(2):
            a = half_filter(lt, 0, xo, 12 * g, 12)
            t = half_filter(lt, 2, xsum, 12 * g, 12)
            for i in range(12):
                n = 12 * g + i
                lcbuf[pl.ds(2 * n, 8, stride=LANE_T), :] = a[i] + dv[n]
                lcbuf[pl.ds(2 * n + 1, 8, stride=LANE_T), :] = t[i] - a[i] - dv[n + 1]

    def residual(lt):
        lanes = slice(lt * 128, (lt + 1) * 128)
        for chunk in range(3):
            rows = slice(chunk * 128, (chunk + 1) * 128)
            features = pick(one_hot(chunk + 2), emb[:, lanes])
            gate = short(0, 256 + chunk * 128, 128, lanes)
            mixed = (features + gate * lcbuf[rows, :]).astype(BF16)
            mbuf[lt, rows, :] = mixed
            mixed_out[rows, lanes] = mixed

    convolve(0)
    for d in ctx_order:
        ag_copy(1, d).wait_recv()
    for chunk in range(1, 5):
        sbuf[chunk * 128 : (chunk + 1) * 128, :C] = pick(one_hot(chunk), tq[...])
    residual(0)
    e1_send(0)
    convolve(1)
    residual(1)
    e1_send(1)

    def chunk_of(b, z_, p):
        rows = rows_at(0, xl) if p == 2 else pl.ds(p * (T // 2), T // 2)
        return mall.at[b, rows, cols_of(z_, k, 1 - p // 2)]

    def zr_copy(b, s, p):
        piece = chunk_of(b, (z + 8 - s) % 8, p)
        return remote(piece, piece, zr_s.at[b, s, p], zr_r.at[b, s, p], z_peer(1))

    def zl_copy(b, s, p):
        piece = chunk_of(b, (z + s) % 8, p)
        return remote(piece, piece, zl_s.at[b, s, p], zl_r.at[b, s, p], z_peer(-1))

    def sib_copy(b, s, h):
        piece = mall.at[b, rows_at(h, xl), cols_of((z + s) % 8, k, h)]
        return remote(piece, piece, sib_s.at[b, s, h], sib_r.at[b, s, h], core_sib)

    def swap_copy(b, s):
        piece = mall.at[b, rows_at(0, xl), cols_of((z + s) % 8, k, 0)]
        return remote(piece, piece, sw_s.at[b, s], sw_r.at[b, s], x_sib)

    def sib2_copy(b, s):
        piece = mall.at[b, rows_at(0, 1 - xl), cols_of((z + s) % 8, k, 0)]
        return remote(piece, piece, sib_s.at[b, s, 2], sib_r.at[b, s, 2], core_sib)

    def share(b, s, p):
        if p > 0:
            sib_copy(b, s, 2 - p).start()
        if p == 2:
            swap_copy(b, s).start()

    def swap_land(b, s):
        swap_copy(b, s).wait_recv()
        sib2_copy(b, s).start()

    def ring_start(b, h):
        piece = mall.at[b, rows_at(h, xl), cols_of(z, k, h)]
        remote(piece, piece, e1_s.at[0, h], e1_r.at[b, h], core_sib).wait_recv()
        for p in ((2,), (0, 1))[h]:
            zr_copy(b, 0, p).start()
            zl_copy(b, 0, p).start()
        share(b, 0, 2 - h)

    def goes_right(s, p):
        return s < 3 or (s == 3 and p < 2)

    def goes_left(s, p):
        return s < 3 or (s == 3 and p == 2)

    def ring_step(b, s):
        for near in ((0,), (7, 1), (6, 2), (5, 3))[s - 1]:
            swap_land(b, near)
        for p in (2, 0, 1):
            if goes_right(s - 1, p):
                zr_copy(b, s - 1, p).wait_recv()
                if goes_right(s, p):
                    zr_copy(b, s, p).start()
            if goes_left(s - 1, p):
                zl_copy(b, s - 1, p).wait_recv()
                if goes_left(s, p):
                    zl_copy(b, s, p).start()
            if goes_right(s - 1, p):
                share(b, 8 - s, p)
            if goes_left(s - 1, p) and s < 4 or s == 4 and p == 2:
                share(b, s, p)

    odd_z = z % 2
    PAIRS = (
        (z // 2, 0, (1 + 6 * odd_z) % 8),
        ((z // 2 + 3 + 2 * odd_z) % 4, (7 + 2 * odd_z) % 8, (6 + 4 * odd_z) % 8),
        ((z // 2 + 5 - 2 * odd_z) % 4, (2 + 4 * odd_z) % 8, (3 + 2 * odd_z) % 8),
        ((z // 2 + 2) % 4, 4, (5 + 6 * odd_z) % 8),
    )

    def pair_land(b, j):
        for s in PAIRS[j][1:]:
            for h in range(2):
                sib_copy(b, s, h).wait_recv()
            sib2_copy(b, s).wait_recv()

    def unit(b, j):
        pair_land(b, j)
        ys = PAIRS[j][0]
        gain2 = g2[pl.ds(pl.multiple_of((4 * xh + ys) * KD, KD), KD)].reshape(1, KD)
        cols = pl.ds(pl.multiple_of(ys * KD, KD), KD)
        for r in range(3):
            rows = slice(r * 128, (r + 1) * 128)
            part = mall[b, rows, cols].astype(F32)
            squares_ = jnp.broadcast_to(jnp.sum(part * part, axis=1, keepdims=True), (128, 128))
            ssb[b, rows, :] = squares_ if j == 0 else ssb[b, rows, :] + squares_
            xs[b, rows, cols] = (part * gain2).astype(BF16)
        for m in (1, 2):
            lanes = slice(m * C, (m + 1) * C)
            term = dot(xs[b, :, cols], w2all[m, ys])
            pp[b, :, lanes] = term if j == 0 else pp[b, :, lanes] + term

    def project_queries():
        terms = [dot(xs[b], w2all[0].reshape(4 * KD, C)) for b in range(2)]
        for b in range(2):
            pp[b, :, :C] = terms[b]

    def g_copy(b, m):
        if m == 3:
            return remote(sqs.at[b], sqr.at[b], g_s.at[b, m], g_r.at[b, m], x_far)
        return remote(gs.at[b, m], gr.at[b, m], g_s.at[b, m], g_r.at[b, m], x_far)

    def head_cols(m, h):
        return pl.ds(pl.multiple_of(m * C + h * HEAD, HEAD), HEAD)

    def send_half(b, ms):
        for m in ms:
            gs[b, m] = pp[b, :, head_cols(m, 1 - xh)].astype(BF16)
            g_copy(b, m).start()

    def send_squares(b):
        sqs[b] = jnp.transpose(ssb[b, :T, :])[0:1, :]
        g_copy(b, 3).start()

    def row_factor(b):
        g_copy(b, 3).wait_recv()
        other = jnp.transpose(jnp.broadcast_to(sqr[b], (128, T)))
        ssb[b, :T, :] = lax.rsqrt((ssb[b, :T, :] + other) / D + EPS)

    def head_norm(values):
        values = values.astype(F32)
        return (values * lax.rsqrt(jnp.mean(values * values, axis=1, keepdims=True) + EPS)).astype(BF16)

    def kv_copy(b, d, part):
        block = (kt, vv)[part].at[y, b]
        side = {1: 0, -1: 1}[d]
        return remote(block, block, kv_s.at[b, part, side], kv_r.at[b, part, side], y_peer(d))

    def kv_forward(b, d):
        side = {1: 0, -1: 1}[d]
        part = (kt, vv)[side].at[(y + 4 - d) % 4, b]
        return remote(part, part, kv_s.at[b, 2, side], kv_r.at[b, 2, side], y_peer(d))

    def kv_pass(b):
        for d in (1, -1):
            kv_copy(b, d, 0 if d == 1 else 1).wait_recv()
            kv_forward(b, d).start()
        for d in (1, -1):
            kv_copy(b, d, 1 if d == 1 else 0).wait_recv()

    def kv_land(b):
        for d in (1, -1):
            kv_forward(b, d).wait_recv()

    def joined(b, m):
        g_copy(b, m).wait_recv()
        return ((pp[b, :, head_cols(m, xh)] + gr[b, m].astype(F32)) * ssb[b, :T, :]).astype(BF16)

    def finish_kv(b):
        row_factor(b)
        kt[y, b] = jnp.transpose(head_norm(joined(b, 1)))
        vv[y, b] = joined(b, 2)
        for part in range(2):
            for d in (1, -1):
                kv_copy(b, d, part).start()

    def finish_q(b):
        qbuf[b] = head_norm(joined(b, 0))

    ring_start(0, 0)
    ring_start(0, 1)
    ring_step(0, 1)
    ring_start(1, 0)
    ring_start(1, 1)
    ring_step(0, 2)
    w_pass(1)
    w_send(2)
    ring_step(0, 3)
    ring_step(1, 1)
    w_send(3)
    ring_step(0, 4)
    ring_step(1, 2)
    w_local.wait()
    w_land(0)
    w_land(1)
    unit(0, 0)
    swap_land(0, 4)
    unit(0, 1)
    unit(0, 2)
    ring_step(1, 3)
    w_pass(2)
    unit(0, 3)
    send_squares(0)
    send_half(0, (1, 2))
    unit(1, 0)
    ring_step(1, 4)
    unit(1, 1)
    w_pass(3)
    swap_land(1, 4)
    finish_kv(0)
    unit(1, 2)
    unit(1, 3)
    send_squares(1)
    send_half(1, (1, 2))
    w_land(2)
    w_land(3)
    project_queries()
    send_half(0, (0,))
    kv_pass(0)
    finish_kv(1)
    send_half(1, (0,))
    finish_q(0)
    kv_land(0)

    factor = 2.0 * HEAD ** -0.5 * math.log2(math.e)

    def key_block(b, ys, kb, diagonal=False, first=False):
        for qc in range(3):
            rows = slice(qc * 128, (qc + 1) * 128)
            width = (qc + 1) * 128 if diagonal else T
            score = dot(qbuf[b, rows, :], kt[ys, kb, :, :width])
            weight = jnp.exp2(score * factor)
            if diagonal:
                at = qc * 128 + lax.broadcasted_iota(jnp.int32, (128, width), 0)
                key = lax.broadcasted_iota(jnp.int32, (128, width), 1)
                weight = jnp.where(key <= at, weight, 0.0)
            part = weight[:, :128]
            for n in range(1, width // 128):
                part = part + weight[:, n * 128 : (n + 1) * 128]
            term = dot(weight.astype(BF16), vv[ys, kb, :width, :])
            if first:
                den[b, rows, :] = part
                num[b, rows, :] = term
            else:
                den[b, rows, :] += part
                num[b, rows, :] += term

    def earlier(b):
        @pl.loop(0, y)
        def _(ys):
            key_block(b, ys, b)

    def o_copy(b, chunk):
        rows = slice(chunk * 128, (chunk + 1) * 128)
        return remote(oloc.at[b, rows, :], obuf.at[rows, :], o_s.at[chunk], o_r.at[chunk], x_far)

    here = pl.ds(pl.multiple_of(xh * HEAD, HEAD), HEAD)
    there = pl.ds(pl.multiple_of((1 - xh) * HEAD, HEAD), HEAD)

    def conclude(b):
        for chunk in range(3):
            rows = slice(chunk * 128, (chunk + 1) * 128)
            out = num[b, rows, :] / jnp.sum(den[b, rows, :], axis=1, keepdims=True)
            oloc[b, rows, :] = out.astype(BF16)

            @pl.when(xh == 1 - b)
            def _():
                o_copy(b, chunk).start()

            @pl.when(xh == b)
            def _():
                att_out[rows, here] = oloc[b, rows, :]

    key_block(0, y, 0, diagonal=True, first=True)
    earlier(0)
    conclude(0)
    kv_pass(1)
    finish_q(1)
    key_block(1, 0, 0, first=True)

    @pl.loop(1, 4)
    def _(ys):
        key_block(1, ys, 0)

    key_block(1, y, 1, diagonal=True)
    kv_land(1)
    earlier(1)
    conclude(1)
    for chunk in range(3):
        o_copy(0, chunk).wait_recv()
    att_out[:, there] = obuf[...]

    @pl.when(c < 7)
    def _():
        id_copy().wait_send()

    for e in range(2):
        same, _, _, cp = sc_copy(e)

        @pl.when(jnp.logical_not(same))
        def _():
            cp.wait_send()

    for a in range(2):
        me = (xl == xh) & (xl == a)

        @pl.when(jnp.logical_not(me))
        def _():
            for h in range(2):
                e1_copy(a, h)[2].wait_send()

    for part in range(4):
        for d in (1, -1):
            w_copy(part, d).wait_send()
            w_forward(part, d).wait_send()
    for d in order:
        az_copy(d).wait_send()
    for d in (0,) + order:
        ax_copy(d).wait_send()
        ac_copy(d, 0).wait_send()
        ac_copy(d, 1).wait_send()
    for d in range(1, 8):
        for kind in range(2):
            ag_copy(kind, d).wait_send()
    for hv in range(2):
        rs_each(hv, range(3), lambda copy: copy.wait_send())
    for b in range(2):
        for s in range(4):
            for p in range(3):
                if goes_right(s, p):
                    zr_copy(b, s, p).wait_send()
                if goes_left(s, p):
                    zl_copy(b, s, p).wait_send()
        for s in range(8):
            for h in range(2):
                sib_copy(b, s, h).wait_send()
            sib2_copy(b, s).wait_send()
            swap_copy(b, s).wait_send()
        for m in range(4):
            g_copy(b, m).wait_send()
        for d in (1, -1):
            for part in range(2):
                kv_copy(b, d, part).wait_send()
            kv_forward(b, d).wait_send()
    for chunk in range(3):
        o_copy(0, chunk).wait_send()


def hand_over(mixed, att, mixed_out, att_out):
    mixed_out[...] = mixed[...]
    att_out[...] = att[...]


def local(base_ids, embedding, first_gain, hyena_weight, short_filter, long_filter, second_gain, attn_weight):
    dma = pltpu.SemaphoreType.DMA
    vmem = pltpu.VMEM
    scratch = [
        vmem((T,), jnp.int32),
        vmem((2, V, 2 * C), BF16),
        vmem((256, KD), BF16),
        vmem((V, 2 * C), BF16),
        vmem((V, C), BF16),
        vmem((2, 1, 256), F32),
        vmem((8, 64, 2 * C), BF16),
        vmem((8, 64, C), BF16),
        vmem((8, 1, 256), F32),
        vmem((V, 2 * C), BF16),
        vmem((V, C), BF16),
        vmem((640, 3 * C), F32),
        vmem((2, 512, 128), F32),
        vmem((LONG, 128), F32),
        vmem((2, 3, LONG // 2, 128), F32),
        vmem((88, 8, 128), F32),
        vmem((88, 8, 128), F32),
        vmem((88, 8, 128), F32),
        vmem((25, 8, 128), F32),
        vmem((T, 128), F32),
        vmem((2, T, 128), BF16),
        vmem((3, 4, KD, C), BF16),
        vmem((2, T, 16 * C), BF16),
        vmem((2, T, 16 * C), BF16),
        vmem((2, T, 3 * C), F32),
        vmem((2, V, 128), F32),
        vmem((2, 3, T, HEAD), BF16),
        vmem((2, 3, T, HEAD), BF16),
        vmem((2, 1, T), F32),
        vmem((2, 1, T), F32),
        vmem((2, T, HEAD), BF16),
        vmem((4, 2, HEAD, T), BF16),
        vmem((4, 2, T, HEAD), BF16),
        vmem((2, T, HEAD), F32),
        vmem((2, T, HEAD), F32),
        vmem((2, T, HEAD), BF16),
        vmem((T, HEAD), BF16),
        dma, dma,
        dma((2,)), dma((2,)),
        dma((8,)), dma((8,)),
        dma((8,)), dma((8,)),
        dma((2, 8)), dma((2, 8)),
        dma((3, 2, 4)), dma((3, 8)),
        dma((2, 7)), dma((2, 7)),
        dma((4, 2, 2)), dma((4, 2, 2)), dma,
        dma((2, 2)), dma((2, 2)),
        dma((2, 4, 3)), dma((2, 4, 3)),
        dma((2, 4, 3)), dma((2, 4, 3)),
        dma((2, 8)), dma((2, 8)),
        dma((2, 8, 3)), dma((2, 8, 3)),
        dma((2, 4)), dma((2, 4)),
        dma((2, 3, 2)), dma((2, 3, 2)),
        dma((3,)), dma((3,)),
    ]
    results = pl.pallas_call(
        kernel,
        out_shape=(jax.ShapeDtypeStruct((T, C), BF16), jax.ShapeDtypeStruct((T, C), BF16)),
        in_specs=[pl.BlockSpec(memory_space=pltpu.VMEM)] * 8,
        out_specs=(pl.BlockSpec(memory_space=pltpu.VMEM), pl.BlockSpec(memory_space=pltpu.VMEM)),
        scratch_shapes=scratch,
        compiler_params=pltpu.CompilerParams(
            collective_id=0, has_side_effects=True, vmem_limit_bytes=56 << 20
        ),
    )(
        base_ids,
        embedding,
        first_gain,
        jnp.transpose(hyena_weight, (1, 0, 2)),
        short_filter,
        long_filter,
        second_gain,
        jnp.transpose(attn_weight, (1, 0, 2)),
    )
    shape = jax.ShapeDtypeStruct((T, C), BF16)
    return pl.pallas_call(hand_over, out_shape=(shape, shape))(*results)


def solution(mesh):
    return jax.shard_map(
        local,
        mesh=mesh,
        in_specs=(
            P("ctx"),
            P(None, "fsdp"),
            P(),
            P("ctx", None, "fsdp"),
            P(None, None, "fsdp"),
            P(None, "fsdp"),
            P(),
            P("ctx", None, "fsdp"),
        ),
        out_specs=(P("ctx", "fsdp"), P("ctx", "fsdp")),
        check_vma=False,
    )
```
